512 devices in a mesh: member: 32 (over y, z_lo), patch: 16 (over z_hi, x, core).
Axes of the slice: x: 4, y: 8, z: 8 (z_hi: 2, z_lo: 4; z = z_hi * 4 + z_lo), core: 2. Of those that a mesh axis runs over, the one named last changes fastest.
Arguments:
- state_field: bfloat16 [32, 16, 256, 512], P('member', None, 'patch'), may hold values from -6 to 6
- cotangent: bfloat16 [32, 16, 256, 512], P('member', None, 'patch'), may hold values from -6 to 6
- obs_count: int32 [16, 256], P(None, 'patch'), may hold values from 0 to 4
- member_gain: float32 [512], replicated, may hold values from 0.5 to 1.5
- spatial_gain: float32 [512], replicated, may hold values from 0.5 to 1.5
- member_weights: bfloat16 [4, 512, 512], replicated, may hold values from -1 to 1
- spatial_weights: bfloat16 [4, 512, 512], replicated, may hold values from -1 to 1
Outputs:
- field_grad: bfloat16 [32, 16, 256, 512], P('member', None, 'patch')
The draws below stay inside these ranges and needn't reach their ends.
All inputs are finite; a program needn't handle non-finite values.
Results may differ from the reference program's by a relative error of at most 0.025.
Values may be sent and summed in bfloat16 or wider, within the bound.
No kernel may reach another device: no remote copies, remote signals or barrier semaphores. Data moves between devices by JAX's collectives and lax.ppermute only.
A program may use at most 64 MiB of HBM per device.

```python
import jax
import jax.numpy as jnp
from jax import lax

D = 512
HEADS = 8
HD = 64
WIN = 8
LAT = 16
MEMBERS = 32
LON = 256


def draw_member_weights(key, part):
    key = jax.random.fold_in(key, 11)
    base = jax.random.normal(key, (4, D, D), jnp.float32) * D ** (-0.5)
    stacked = jnp.stack([base[0], base[1], base[2], 5.0 * base[3]])
    return jnp.clip(stacked, -1.0, 1.0).astype(jnp.bfloat16)


def draw_spatial_weights(key, part):
    key = jax.random.fold_in(key, 23)
    stacked = jax.random.normal(key, (4, D, D), jnp.float32) * D ** (-0.5)
    return jnp.clip(stacked, -1.0, 1.0).astype(jnp.bfloat16)


def set_ends(array, own_key, least, largest):
    shape = array.shape
    spot = [jax.random.randint(jax.random.fold_in(own_key, axis), (), 0, shape[axis]) for axis in range(len(shape))]
    array = array.at[tuple(spot)].set(least)
    longest = shape.index(max(shape))
    spot[longest] = (spot[longest] + 1) % shape[longest]
    return array.at[tuple(spot)].set(largest)


def steps_of(stream_key, extent, cuts, low, largest):
    level = 1.0
    for dim, blocks in cuts:
        steps = jax.random.uniform(jax.random.fold_in(jax.random.fold_in(stream_key, 6), dim), (blocks,), jnp.float32, low / len(cuts), largest / len(cuts))
        level = level * jnp.repeat(jnp.exp(steps), extent[dim] // blocks).reshape((-1,) + (1,) * (len(extent) - 1 - dim))
    return level


def scatter_about(rng, dims, scale, reach, pieces=(), dtype=jnp.bfloat16):
    result = jax.random.normal(rng, dims, jnp.float32) * scale
    if len(pieces) > 0:
        result = steps_of(rng, dims, pieces, -0.22, 0.18) * result
    return jnp.clip(result, min=-reach, max=reach).astype(dtype)


def setup_inputs(seed: int = 0) -> dict:
    streams_of = jax.random.split(jax.random.key(seed), 8)
    return {
        "state_field": scatter_about(streams_of[0], (MEMBERS, LAT, LON, D), 1.0, 6.0, ((0, 32), (2, 16))),
        "cotangent": scatter_about(streams_of[1], (MEMBERS, LAT, LON, D), 1.0, 6.0, ((0, 32), (2, 16))),
        "obs_count": set_ends(jax.random.randint(streams_of[2], (LAT, LON), 0, 5), jax.random.fold_in(streams_of[2], 1), 0, 4).astype(jnp.int32),
        "member_gain": jnp.clip(1.0 + 0.1 * jax.random.normal(streams_of[3], (D,), jnp.float32), 0.5, 1.5),
        "spatial_gain": jnp.clip(1.0 + 0.1 * jax.random.normal(streams_of[4], (D,), jnp.float32), 0.5, 1.5),
        "member_weights": draw_member_weights(jax.random.fold_in(streams_of[7], 71), 0),
        "spatial_weights": draw_spatial_weights(jax.random.fold_in(streams_of[7], 71), 0),
    }


epsilon = 1e-06

def rms_norm(activity, scaling):
    values = activity.astype(jnp.float32)
    inverse = lax.rsqrt(lax.optimization_barrier(jnp.mean(values * values, axis=-1, keepdims=True)) + epsilon)
    return (values * inverse * scaling).astype(jnp.bfloat16)

def norm_back(activity, scaling, upstream):
    values = activity.astype(jnp.float32)
    inverse = lax.rsqrt(lax.optimization_barrier(jnp.mean(values * values, axis=-1, keepdims=True)) + epsilon)
    scaled = scaling * upstream
    inner_mean = lax.optimization_barrier(jnp.mean(scaled * values, axis=-1, keepdims=True))
    return inverse * scaled - values * inverse * inverse * inverse * inner_mean

def project(activity, matrix):
    return jnp.dot(activity, matrix, preferred_element_type=jnp.float32)

def project_back(activity, matrix):
    return jnp.dot(activity, matrix.T, preferred_element_type=jnp.float32)

def round_keep(values):
    return lax.optimization_barrier(values.astype(jnp.bfloat16)).astype(jnp.float32)

def attention_probs(query_rows, key_rows):
    scores = jnp.einsum('bqhe,bkhe->bhqk', query_rows.astype(jnp.float32), key_rows.astype(jnp.float32)) * HD ** (-0.5)
    return jax.nn.softmax(scores, axis=-1)

def attend_forward(query_rows, key_rows, value_rows):
    rounded = round_keep(attention_probs(query_rows, key_rows))
    return jnp.einsum('bhqk,bkhe->bqhe', rounded, value_rows.astype(jnp.float32)).astype(jnp.bfloat16)

def attend_back(query_rows, key_rows, value_rows, output_grad):
    probs_full = attention_probs(query_rows, key_rows)
    rounded = round_keep(probs_full)
    grad_full = output_grad.astype(jnp.float32)
    prob_grad = jnp.einsum('bqhe,bkhe->bhqk', grad_full, value_rows.astype(jnp.float32))
    value_grad = jnp.einsum('bhqk,bqhe->bkhe', rounded, grad_full)
    score_grad = probs_full * (prob_grad - lax.optimization_barrier(jnp.sum(probs_full * prob_grad, axis=-1, keepdims=True)))
    score_low = round_keep(score_grad * HD ** (-0.5))
    query_grad = jnp.einsum('bhqk,bkhe->bqhe', score_low, key_rows.astype(jnp.float32))
    key_grad = jnp.einsum('bhqk,bqhe->bkhe', score_low, query_rows.astype(jnp.float32))
    return (query_grad, key_grad, value_grad)

def to_points(activity):
    member_count, row_count, col_count, feature_count = activity.shape
    shaped = activity.reshape(member_count, row_count * col_count, HEADS, feature_count // HEADS)
    return shaped.transpose(1, 0, 2, 3)

def from_points(blocks, row_count, col_count):
    point_count, member_count, head_count, head_size = blocks.shape
    shaped = blocks.transpose(1, 0, 2, 3)
    return shaped.reshape(member_count, row_count, col_count, head_count * head_size)

def to_windows(activity):
    member_count, row_count, col_count, feature_count = activity.shape
    rolled = jnp.roll(activity, -(WIN // 2), axis=2)
    shaped = rolled.reshape(member_count, row_count // WIN, WIN, col_count // WIN, WIN, HEADS, feature_count // HEADS)
    return shaped.transpose(0, 1, 3, 2, 4, 5, 6).reshape(-1, WIN * WIN, HEADS, feature_count // HEADS)

def from_windows(blocks, member_count, row_count, col_count):
    head_count, head_size = (blocks.shape[2], blocks.shape[3])
    shaped = blocks.reshape(member_count, row_count // WIN, col_count // WIN, WIN, WIN, head_count, head_size)
    shaped = shaped.transpose(0, 1, 3, 2, 4, 5, 6).reshape(member_count, row_count, col_count, head_count * head_size)
    return jnp.roll(shaped, WIN // 2, axis=2)

def reference(state_field, cotangent, obs_count, member_gain, spatial_gain, member_weights, spatial_weights):
    member_count, row_count, col_count, feature_count = state_field.shape
    normed_one = rms_norm(state_field, member_gain)
    query_one = project(normed_one, member_weights[0]).astype(jnp.bfloat16)
    key_one = project(normed_one, member_weights[1]).astype(jnp.bfloat16)
    value_one = project(normed_one, member_weights[2]).astype(jnp.bfloat16)
    attended = attend_forward(to_points(query_one), to_points(key_one), to_points(value_one))
    attended = from_points(attended, row_count, col_count)
    hidden = (state_field.astype(jnp.float32) + project(attended, member_weights[3])).astype(jnp.bfloat16)
    normed_two = rms_norm(hidden, spatial_gain)
    query_two = project(normed_two, spatial_weights[0]).astype(jnp.bfloat16)
    key_two = project(normed_two, spatial_weights[1]).astype(jnp.bfloat16)
    value_two = project(normed_two, spatial_weights[2]).astype(jnp.bfloat16)
    weighting = obs_count.astype(jnp.float32)[None, :, :, None]
    out_grad = (cotangent.astype(jnp.float32) * weighting).astype(jnp.bfloat16)
    attn_grad_two = project_back(out_grad, spatial_weights[3]).astype(jnp.bfloat16)
    grads_two = attend_back(to_windows(query_two), to_windows(key_two), to_windows(value_two), to_windows(attn_grad_two))
    grads_two = [from_windows(piece, member_count, row_count, col_count).astype(jnp.bfloat16) for piece in grads_two]
    normed_grad_two = project_back(grads_two[0], spatial_weights[0]) + project_back(grads_two[1], spatial_weights[1]) + project_back(grads_two[2], spatial_weights[2])
    hidden_grad = (out_grad.astype(jnp.float32) + norm_back(hidden, spatial_gain, normed_grad_two)).astype(jnp.bfloat16)
    attn_grad_one = project_back(hidden_grad, member_weights[3]).astype(jnp.bfloat16)
    grads_one = attend_back(to_points(query_one), to_points(key_one), to_points(value_one), to_points(attn_grad_one))
    grads_one = [from_points(piece.astype(jnp.bfloat16), row_count, col_count) for piece in grads_one]
    normed_grad_one = project_back(grads_one[0], member_weights[0]) + project_back(grads_one[1], member_weights[1]) + project_back(grads_one[2], member_weights[2])
    return (hidden_grad.astype(jnp.float32) + norm_back(state_field, member_gain, normed_grad_one)).astype(jnp.bfloat16)
```

```python
import jax
import jax.numpy as jnp
from jax import lax
from jax.experimental import pallas as pl
from jax.experimental.pallas import tpu as pltpu
from jax.sharding import PartitionSpec as P

F32 = jnp.float32
BF16 = jnp.bfloat16
D = 512
PAIRS = 4
SCALE = 64 ** (-0.5)
EPS = 1e-6
ROWS = 256
BLOCK = 128

NN = (((1,), (0,)), ((), ()))
NT = (((1,), (1,)), ((), ()))
TN = (((0,), (0,)), ((), ()))


def dot(a, b, dims=NN):
    return lax.dot_general(a, b, dims, preferred_element_type=F32)


def inverse_rms(values):
    return lax.rsqrt(jnp.mean(values * values, axis=-1, keepdims=True) + EPS)


def norm_back(values, inverse, gain, upstream):
    scaled = gain * upstream
    inner = jnp.mean(scaled * values, axis=-1, keepdims=True)
    return inverse * scaled - values * (inverse * inverse * inverse * inner)


def cell_major():
    to = lax.broadcasted_iota(jnp.int32, (ROWS, ROWS), 0)
    at = lax.broadcasted_iota(jnp.int32, (ROWS, ROWS), 1)
    return (at == (to % 32) * 8 + to // 32).astype(F32).astype(BF16)


def member_major():
    to = lax.broadcasted_iota(jnp.int32, (ROWS, ROWS), 0)
    at = lax.broadcasted_iota(jnp.int32, (ROWS, ROWS), 1)
    return (at == (to % 8) * 32 + to // 8).astype(F32).astype(BF16)


def head_split(rows):
    first = lax.broadcasted_iota(jnp.int32, rows.shape, 1) < 64
    zero = jnp.zeros_like(rows)
    return jnp.concatenate([jnp.where(first, rows, zero), jnp.where(first, zero, rows)], axis=0)


def head_join(stacked):
    first = lax.broadcasted_iota(jnp.int32, (BLOCK, 128), 1) < 64
    return jnp.where(first, stacked[:BLOCK], stacked[BLOCK:])


def own_group(width, size):
    return (lax.broadcasted_iota(jnp.int32, (size, width), 1) % BLOCK) // size


def compact(full, size):
    group = own_group(full.shape[1], size)
    kept = full[:size]
    for g in range(1, BLOCK // size):
        kept = jnp.where(group == g, full[g * size : (g + 1) * size], kept)
    return kept


def expand(kept, size):
    group = own_group(kept.shape[1], size)
    zero = jnp.zeros_like(kept)
    return jnp.concatenate(
        [jnp.where(group == g, kept, zero) for g in range(BLOCK // size)], axis=0
    ).astype(BF16)


def softmax_keys(scores):
    raised = jnp.exp(scores - jnp.max(scores, axis=0, keepdims=True))
    return raised * (1.0 / jnp.sum(raised, axis=0, keepdims=True))


def block_backward(probs, q_two, k, v, do_two, size):
    grad = compact(dot(v, do_two, NT), size)
    inner = jnp.sum(probs * grad, axis=0, keepdims=True)
    ds = expand(probs * (grad - inner) * SCALE, size)
    dv = dot(expand(probs, size), do_two)
    dk = dot(ds, q_two)
    dq = head_join(dot(ds, k, TN))
    return dq, dk, dv


def spread_kernel(state_ref, cot_ref, obs_ref, out_ref):
    obs = obs_ref[...].astype(F32)
    eye = lax.broadcasted_iota(jnp.int32, (16, 16, 16), 1) == lax.broadcasted_iota(
        jnp.int32, (16, 16, 16), 2
    )
    weight = jnp.sum(jnp.where(eye, obs[:, None, :], 0.0), axis=-1, keepdims=True)
    dy = cot_ref[...].astype(F32) * weight
    parts = []
    for values in (state_ref[...].astype(F32), dy):
        inner = values[:, 4:12]
        west = values[:, 0:4].reshape(8, 2, 4, D)
        east = values[:, 12:16].reshape(8, 2, 4, D)
        parts.append(
            [
                jnp.concatenate([west[:, 0], west[:, 1]], axis=1),
                inner,
                jnp.concatenate([east[:, 0], east[:, 1]], axis=1),
            ]
        )
    for at, size, a, b in zip((0, 8, 24), (8, 16, 8), parts[0], parts[1]):
        out_ref[at : at + size] = jnp.concatenate([a, b], axis=1).astype(BF16)


def gather_kernel(in_ref, out_ref):
    values = in_ref[...].astype(F32)
    west, east = values[0:8], values[24:32]
    inner = values[8:24].reshape(8, 2, 8, D)
    rows = [
        jnp.concatenate([west[:, 4 * i : 4 * i + 4], inner[:, i], east[:, 4 * i : 4 * i + 4]], axis=1)
        for i in range(2)
    ]
    out_ref[...] = jnp.stack(rows, axis=1).reshape(16, 16, D).astype(BF16)


def member_forward_kernel(
    in_ref, gain_ref, w_ref, out_ref, state_ref, q_ref, k_ref, v_ref, probs_ref, attended_ref
):
    values = in_ref[...].astype(F32)
    state = dot(cell_major(), values[:, :8].reshape(ROWS, D).astype(BF16))
    state_ref[...] = state.astype(BF16)
    normed = (state * inverse_rms(state) * gain_ref[...]).astype(BF16)
    q_ref[...] = dot(normed, w_ref[0]).astype(BF16)
    k_ref[...] = dot(normed, w_ref[1]).astype(BF16)
    v_ref[...] = dot(normed, w_ref[2]).astype(BF16)
    for b in range(2):
        rows = slice(b * BLOCK, (b + 1) * BLOCK)
        for p in range(PAIRS):
            cols = slice(p * 128, (p + 1) * 128)
            scores = compact(dot(k_ref[rows, cols], head_split(q_ref[rows, cols]), NT), 32) * SCALE
            probs = softmax_keys(scores)
            probs_ref[b * PAIRS + p] = probs
            attended = head_join(dot(expand(probs, 32), v_ref[rows, cols], TN))
            attended_ref[rows, cols] = attended.astype(BF16)
    hidden = (state + dot(attended_ref[...], w_ref[3])).astype(BF16)
    hidden = dot(member_major(), hidden).reshape(32, 8, D)
    out_ref[...] = jnp.concatenate([hidden, values[:, 8:]], axis=1).astype(BF16).reshape(8, 4, 16, D)


def window_kernel(
    in_ref, gain_ref, w_ref, out_ref, q_ref, k_ref, v_ref, do_ref, dq_ref, dk_ref, dv_ref
):
    values = in_ref[...].astype(F32)
    hidden = jnp.concatenate([values[:, m, :8].reshape(64, D) for m in range(4)], axis=0)
    dy = jnp.concatenate([values[:, m, 8:].reshape(64, D) for m in range(4)], axis=0)
    inverse = inverse_rms(hidden)
    normed = (hidden * inverse * gain_ref[...]).astype(BF16)
    q_ref[...] = dot(normed, w_ref[0]).astype(BF16)
    k_ref[...] = dot(normed, w_ref[1]).astype(BF16)
    v_ref[...] = dot(normed, w_ref[2]).astype(BF16)
    do_ref[...] = dot(dy.astype(BF16), w_ref[3], NT).astype(BF16)
    for b in range(2):
        rows = slice(b * BLOCK, (b + 1) * BLOCK)
        for p in range(PAIRS):
            cols = slice(p * 128, (p + 1) * 128)
            q_two, do_two = head_split(q_ref[rows, cols]), head_split(do_ref[rows, cols])
            k, v = k_ref[rows, cols], v_ref[rows, cols]
            probs = softmax_keys(compact(dot(k, q_two, NT), 64) * SCALE)
            dq, dk, dv = block_backward(probs, q_two, k, v, do_two, 64)
            dq_ref[rows, cols] = dq.astype(BF16)
            dk_ref[rows, cols] = dk.astype(BF16)
            dv_ref[rows, cols] = dv.astype(BF16)
    upstream = (
        dot(dq_ref[...], w_ref[0], NT) + dot(dk_ref[...], w_ref[1], NT) + dot(dv_ref[...], w_ref[2], NT)
    )
    grad = dy + norm_back(hidden, inverse, gain_ref[...], upstream)
    for m in range(4):
        out_ref[:, m] = grad[m * 64 : (m + 1) * 64].reshape(8, 8, D).astype(BF16)


def member_backward_kernel(
    in_ref, state_ref, q_ref, k_ref, v_ref, probs_ref, gain_ref, w_ref, out_ref, do_ref, dq_ref, dk_ref, dv_ref
):
    values = in_ref[...].astype(F32).reshape(ROWS, D).astype(BF16)
    hidden_grad = dot(cell_major(), values)
    do_ref[...] = dot(hidden_grad.astype(BF16), w_ref[3], NT).astype(BF16)
    for b in range(2):
        rows = slice(b * BLOCK, (b + 1) * BLOCK)
        for p in range(PAIRS):
            cols = slice(p * 128, (p + 1) * 128)
            q_two, do_two = head_split(q_ref[rows, cols]), head_split(do_ref[rows, cols])
            dq, dk, dv = block_backward(
                probs_ref[b * PAIRS + p], q_two, k_ref[rows, cols], v_ref[rows, cols], do_two, 32
            )
            dq_ref[rows, cols] = dq.astype(BF16)
            dk_ref[rows, cols] = dk.astype(BF16)
            dv_ref[rows, cols] = dv.astype(BF16)
    upstream = (
        dot(dq_ref[...], w_ref[0], NT) + dot(dk_ref[...], w_ref[1], NT) + dot(dv_ref[...], w_ref[2], NT)
    )
    state = state_ref[...].astype(F32)
    grad = (hidden_grad + norm_back(state, inverse_rms(state), gain_ref[...], upstream)).astype(BF16)
    out_ref[...] = dot(member_major(), grad).astype(BF16).reshape(32, 8, D)


def call(kernel, outs, scratch=(), flops=0):
    return pl.pallas_call(
        kernel,
        out_shape=outs,
        scratch_shapes=[pltpu.VMEM(s, t) for s, t in scratch],
        compiler_params=pltpu.CompilerParams(vmem_limit_bytes=32 * 1024 * 1024),
    )


def shape(dims, dtype=BF16):
    return jax.ShapeDtypeStruct(dims, dtype)


def member_order():
    def at(y, z):
        return y * 4 + z

    return (
        [at(y, 0) for y in range(8)]
        + [at(y, z) for z in (1, 2) for y in range(4)]
        + [at(y, z) for z in (1, 2) for y in range(4, 8)]
        + [at(y, 3) for y in range(8)]
    )


def groups(patches):
    order = member_order()
    cells = [[m * patches + p for m in order] for p in range(patches)]
    windows = []
    for p in range(patches):
        here, east = cells[p], cells[(p + 1) % patches]
        windows += [here[8:16], here[16:24]]
        windows += [here[24:28] + east[0:4], here[28:32] + east[4:8]]
    return cells, windows


def exchange(array, parties):
    return lax.all_to_all(
        array, ("member", "patch"), 0, 0, axis_index_groups=parties, tiled=True
    )


def body(
    state_field, cotangent, obs_count, member_gain, spatial_gain, member_weights, spatial_weights
):
    cells, windows = groups(lax.axis_size("patch"))
    member_gain, spatial_gain = member_gain.reshape(1, D), spatial_gain.reshape(1, D)
    rows = (ROWS, D)
    sent = call(spread_kernel, shape((32, 16, D)))(
        state_field.reshape(16, 16, D), cotangent.reshape(16, 16, D), obs_count
    )
    at_cells = exchange(sent, cells)
    hidden, state, q, k, v, probs = call(
        member_forward_kernel,
        [shape((8, 4, 16, D))] + [shape(rows)] * 4 + [shape((8, 32, 256), F32)],
        [(rows, BF16)],
    )(at_cells, member_gain, member_weights)
    at_windows = exchange(hidden, windows)
    grads = call(window_kernel, shape((8, 4, 8, D)), [(rows, BF16)] * 7)(
        at_windows, spatial_gain, spatial_weights
    )
    back_at_cells = exchange(grads, windows)
    field = call(member_backward_kernel, shape((32, 8, D)), [(rows, BF16)] * 4)(
        back_at_cells, state, q, k, v, probs, member_gain, member_weights
    )
    returned = exchange(field, cells)
    out = call(gather_kernel, shape((16, 16, D)))(returned)
    return out.reshape(1, 16, 16, D)


def solution(mesh):
    placed = (
        P("member", None, "patch", None),
        P("member", None, "patch", None),
        P(None, "patch"),
        P(),
        P(),
        P(),
        P(),
    )
    return jax.shard_map(
        body,
        mesh=mesh,
        in_specs=placed,
        out_specs=P("member", None, "patch", None),
        check_vma=False,
    )
```

```python
import jax
import jax.numpy as jnp
from jax import lax
from jax.experimental import pallas as pl
from jax.experimental.pallas import tpu as pltpu
from jax.sharding import PartitionSpec as P

F32 = jnp.float32
BF16 = jnp.bfloat16
D = 512
PAIRS = 4
SCALE = 64 ** (-0.5)
EPS = 1e-6
ROWS = 256
BLOCK = 128

NN = (((1,), (0,)), ((), ()))
NT = (((1,), (1,)), ((), ()))
TN = (((0,), (0,)), ((), ()))


def dot(a, b, dims=NN):
    return lax.dot_general(a, b, dims, preferred_element_type=F32)


def inverse_rms(values):
    return lax.rsqrt(jnp.mean(values * values, axis=-1, keepdims=True) + EPS)


def norm_back(values, inverse, gain, upstream):
    scaled = gain * upstream
    inner = jnp.mean(scaled * values, axis=-1, keepdims=True)
    return inverse * scaled - values * (inverse * inverse * inverse * inner)


def cell_major():
    to = lax.broadcasted_iota(jnp.int32, (ROWS, ROWS), 0)
    at = lax.broadcasted_iota(jnp.int32, (ROWS, ROWS), 1)
    return (at == (to % 32) * 8 + to // 32).astype(F32).astype(BF16)


def member_major():
    to = lax.broadcasted_iota(jnp.int32, (ROWS, ROWS), 0)
    at = lax.broadcasted_iota(jnp.int32, (ROWS, ROWS), 1)
    return (at == (to % 8) * 32 + to // 8).astype(F32).astype(BF16)


def head_split(rows):
    first = lax.broadcasted_iota(jnp.int32, rows.shape, 1) < 64
    zero = jnp.zeros_like(rows)
    return jnp.concatenate([jnp.where(first, rows, zero), jnp.where(first, zero, rows)], axis=0)


def head_join(stacked):
    first = lax.broadcasted_iota(jnp.int32, (BLOCK, 128), 1) < 64
    return jnp.where(first, stacked[:BLOCK], stacked[BLOCK:])


def own_group(width, size):
    return (lax.broadcasted_iota(jnp.int32, (size, width), 1) % BLOCK) // size


def compact(full, size):
    group = own_group(full.shape[1], size)
    kept = full[:size]
    for g in range(1, BLOCK // size):
        kept = jnp.where(group == g, full[g * size : (g + 1) * size], kept)
    return kept


def expand(kept, size):
    group = own_group(kept.shape[1], size)
    zero = jnp.zeros_like(kept)
    return jnp.concatenate(
        [jnp.where(group == g, kept, zero) for g in range(BLOCK // size)], axis=0
    ).astype(BF16)


def softmax_keys(scores):
    raised = jnp.exp(scores - jnp.max(scores, axis=0, keepdims=True))
    return raised * (1.0 / jnp.sum(raised, axis=0, keepdims=True))


def blocks():
    return [
        (slice(b * BLOCK, (b + 1) * BLOCK), slice(p * 128, (p + 1) * 128))
        for b in range(ROWS // BLOCK)
        for p in range(PAIRS)
    ]


def attention_probs(q_split, k_ref, size):
    scores = [dot(k_ref[at], q, NT) for at, q in zip(blocks(), q_split)]
    scores = [compact(s, size) * SCALE for s in scores]
    return [softmax_keys(s) for s in scores]


def attention_backward(probs, q_split, k_ref, v_ref, do_split, dq_ref, dk_ref, dv_ref, size):
    grads = [dot(v_ref[at], do, NT) for at, do in zip(blocks(), do_split)]
    grads = [compact(g, size) for g in grads]
    wide = [expand(p, size) for p in probs]
    ds = [
        expand(p * (g - jnp.sum(p * g, axis=0, keepdims=True)) * SCALE, size)
        for p, g in zip(probs, grads)
    ]
    for at, p, do in zip(blocks(), wide, do_split):
        dv_ref[at] = dot(p, do).astype(BF16)
    for at, d, q in zip(blocks(), ds, q_split):
        dk_ref[at] = dot(d, q).astype(BF16)
    for at, d in zip(blocks(), ds):
        dq_ref[at] = head_join(dot(d, k_ref[at], TN)).astype(BF16)


def spread_kernel(state_hbm, cot_hbm, obs_hbm, out_ref, state_ref, cot_ref, obs_ref, sems):
    copies = [
        pltpu.make_async_copy(src, dst, sems.at[i])
        for i, (src, dst) in enumerate(
            ((obs_hbm, obs_ref), (state_hbm, state_ref), (cot_hbm, cot_ref))
        )
    ]
    for copy in copies:
        copy.start()
    for copy in copies:
        copy.wait()
    obs = obs_ref[...].astype(F32)
    eye = lax.broadcasted_iota(jnp.int32, (16, 16, 16), 1) == lax.broadcasted_iota(
        jnp.int32, (16, 16, 16), 2
    )
    weight = jnp.sum(jnp.where(eye, obs[:, None, :], 0.0), axis=-1, keepdims=True)
    dy = cot_ref[...].astype(F32) * weight
    parts = []
    for values in (state_ref[...].astype(F32), dy):
        inner = values[:, 4:12]
        west = values[:, 0:4].reshape(8, 2, 4, D)
        east = values[:, 12:16].reshape(8, 2, 4, D)
        parts.append(
            [
                jnp.concatenate([west[:, 0], west[:, 1]], axis=1),
                inner,
                jnp.concatenate([east[:, 0], east[:, 1]], axis=1),
            ]
        )
    sent = [jnp.concatenate([a, b], axis=1).astype(BF16) for a, b in zip(parts[0], parts[1])]
    for k, block in enumerate(block_order()):
        part, at = (0, block) if block < 8 else (1, block - 8) if block < 24 else (2, block - 24)
        out_ref[k] = sent[part][at]


def gather_kernel(in_ref, out_ref):
    order = block_order()
    values = jnp.stack([in_ref[order.index(block)] for block in range(32)]).astype(F32)
    west, east = values[0:8], values[24:32]
    inner = values[8:24].reshape(8, 2, 8, D)
    rows = [
        jnp.concatenate([west[:, 4 * i : 4 * i + 4], inner[:, i], east[:, 4 * i : 4 * i + 4]], axis=1)
        for i in range(2)
    ]
    out_ref[...] = jnp.stack(rows, axis=1).reshape(16, 16, D).astype(BF16)


def member_forward_kernel(
    in_ref, gain_ref, w_ref, out_ref, state_ref, q_ref, k_ref, v_ref, probs_ref, attended_ref
):
    values = in_ref[...].astype(F32)
    state = dot(cell_major(), values[:, :8].reshape(ROWS, D).astype(BF16))
    state_ref[...] = state.astype(BF16)
    normed = (state * inverse_rms(state) * gain_ref[...]).astype(BF16)
    q_ref[...] = dot(normed, w_ref[0]).astype(BF16)
    k_ref[...] = dot(normed, w_ref[1]).astype(BF16)
    v_ref[...] = dot(normed, w_ref[2]).astype(BF16)
    probs = attention_probs([head_split(q_ref[at]) for at in blocks()], k_ref, 32)
    for i, p in enumerate(probs):
        probs_ref[i] = p
    for at, p in zip(blocks(), probs):
        attended_ref[at] = head_join(dot(expand(p, 32), v_ref[at], TN)).astype(BF16)
    hidden = (state + dot(attended_ref[...], w_ref[3])).astype(BF16)
    hidden = dot(member_major(), hidden).reshape(32, 8, D)
    out_ref[...] = jnp.concatenate([hidden, values[:, 8:]], axis=1).astype(BF16).reshape(8, 4, 16, D)


def window_kernel(
    in_ref, gain_ref, w_ref, out_ref, q_ref, k_ref, v_ref, do_ref, dq_ref, dk_ref, dv_ref
):
    values = in_ref[...].astype(F32)
    hidden = jnp.concatenate([values[:, m, :8].reshape(64, D) for m in range(4)], axis=0)
    dy = jnp.concatenate([values[:, m, 8:].reshape(64, D) for m in range(4)], axis=0)
    inverse = inverse_rms(hidden)
    normed = (hidden * inverse * gain_ref[...]).astype(BF16)
    q_ref[...] = dot(normed, w_ref[0]).astype(BF16)
    k_ref[...] = dot(normed, w_ref[1]).astype(BF16)
    v_ref[...] = dot(normed, w_ref[2]).astype(BF16)
    do_ref[...] = dot(dy.astype(BF16), w_ref[3], NT).astype(BF16)
    q_split = [head_split(q_ref[at]) for at in blocks()]
    do_split = [head_split(do_ref[at]) for at in blocks()]
    probs = attention_probs(q_split, k_ref, 64)
    attention_backward(probs, q_split, k_ref, v_ref, do_split, dq_ref, dk_ref, dv_ref, 64)
    upstream = (
        dot(dq_ref[...], w_ref[0], NT) + dot(dk_ref[...], w_ref[1], NT) + dot(dv_ref[...], w_ref[2], NT)
    )
    grad = dy + norm_back(hidden, inverse, gain_ref[...], upstream)
    for m in range(4):
        out_ref[:, m] = grad[m * 64 : (m + 1) * 64].reshape(8, 8, D).astype(BF16)


def member_backward_kernel(
    in_ref, state_ref, q_ref, k_ref, v_ref, probs_ref, gain_ref, w_ref, out_ref, do_ref, dq_ref, dk_ref, dv_ref
):
    values = in_ref[...].astype(F32).reshape(ROWS, D).astype(BF16)
    hidden_grad = dot(cell_major(), values)
    do_ref[...] = dot(hidden_grad.astype(BF16), w_ref[3], NT).astype(BF16)
    q_split = [head_split(q_ref[at]) for at in blocks()]
    do_split = [head_split(do_ref[at]) for at in blocks()]
    probs = [probs_ref[i] for i in range(len(q_split))]
    attention_backward(probs, q_split, k_ref, v_ref, do_split, dq_ref, dk_ref, dv_ref, 32)
    upstream = (
        dot(dq_ref[...], w_ref[0], NT) + dot(dk_ref[...], w_ref[1], NT) + dot(dv_ref[...], w_ref[2], NT)
    )
    state = state_ref[...].astype(F32)
    grad = (hidden_grad + norm_back(state, inverse_rms(state), gain_ref[...], upstream)).astype(BF16)
    out_ref[...] = dot(member_major(), grad).astype(BF16).reshape(32, 8, D)


def call(kernel, outs, scratch=()):
    return pl.pallas_call(
        kernel,
        out_shape=outs,
        scratch_shapes=[pltpu.VMEM(s, t) for s, t in scratch],
        compiler_params=pltpu.CompilerParams(vmem_limit_bytes=32 * 1024 * 1024),
    )


def shape(dims, dtype=BF16):
    return jax.ShapeDtypeStruct(dims, dtype)


def holders():
    def at(y, z):
        return y * 4 + z

    west = [at(half + y, z) for half in (0, 4) for y in (0, 1) for z in (0, 1)]
    within = [at(half + y, z) for half in (0, 4) for y in (2, 3) for z in range(4)]
    east = [at(half + y, z) for half in (0, 4) for y in (0, 1) for z in (3, 2)]
    return west + within + east


def member_order():
    order = []
    for i in range(32):
        y = (i >> 4 & 1) * 4 + (i >> 3 & 1) * 2 + (i & 1)
        z = (i >> 1 & 1) * 2 + (i >> 2 & 1)
        y, z = y ^ (y >> 1), z ^ (z >> 1)
        order.append(y * 4 + (z + y) % 4)
    return order


def block_order():
    held = holders()
    return [held.index(m) for m in member_order()]


def groups(patches):
    order = member_order()
    cells = [[m * patches + p for m in order] for p in range(patches)]
    held = [[m * patches + p for m in holders()] for p in range(patches)]
    windows = []
    for p in range(patches):
        here, east = held[p], held[(p + 1) % patches]
        windows += [here[8:16], here[16:24]]
        windows += [here[24:28] + east[0:4], here[28:32] + east[4:8]]
    return cells, windows


def exchange(array, parties):
    return lax.all_to_all(
        array, ("member", "patch"), 0, 0, axis_index_groups=parties, tiled=True
    )


def body(
    state_field, cotangent, obs_count, member_gain, spatial_gain, member_weights, spatial_weights
):
    cells, windows = groups(lax.axis_size("patch"))
    member_gain, spatial_gain = member_gain.reshape(1, D), spatial_gain.reshape(1, D)
    rows = (ROWS, D)
    sent = pl.pallas_call(
        spread_kernel,
        out_shape=shape((32, 16, D)),
        in_specs=[pl.BlockSpec(memory_space=pltpu.HBM)] * 3,
        scratch_shapes=[
            pltpu.VMEM((16, 16, D), BF16),
            pltpu.VMEM((16, 16, D), BF16),
            pltpu.VMEM((16, 16), jnp.int32),
            pltpu.SemaphoreType.DMA((3,)),
        ],
    )(state_field.reshape(16, 16, D), cotangent.reshape(16, 16, D), obs_count)
    at_cells = exchange(sent, cells)
    hidden, state, q, k, v, probs = call(
        member_forward_kernel,
        [shape((8, 4, 16, D))] + [shape(rows)] * 4 + [shape((8, 32, 256), F32)],
        [(rows, BF16)],
    )(at_cells, member_gain, member_weights)
    at_windows = exchange(hidden, windows)
    grads = call(window_kernel, shape((8, 4, 8, D)), [(rows, BF16)] * 7)(
        at_windows, spatial_gain, spatial_weights
    )
    back_at_cells = exchange(grads, windows)
    field = call(member_backward_kernel, shape((32, 8, D)), [(rows, BF16)] * 4)(
        back_at_cells, state, q, k, v, probs, member_gain, member_weights
    )
    returned = exchange(field, cells)
    out = call(gather_kernel, shape((16, 16, D)))(returned)
    return out.reshape(1, 16, 16, D)


def solution(mesh):
    placed = (
        P("member", None, "patch", None),
        P("member", None, "patch", None),
        P(None, "patch"),
        P(),
        P(),
        P(),
        P(),
    )
    return jax.shard_map(
        body,
        mesh=mesh,
        in_specs=placed,
        out_specs=P("member", None, "patch", None),
        check_vma=False,
    )
```

```python
import jax
import jax.numpy as jnp
from jax import lax
from jax.experimental import pallas as pl
from jax.experimental.pallas import tpu as pltpu
from jax.sharding import PartitionSpec as P

F32 = jnp.float32
BF16 = jnp.bfloat16
D = 512
PAIRS = 4
SCALE = 64 ** (-0.5)
EPS = 1e-6
ROWS = 256
BLOCK = 128

NN = (((1,), (0,)), ((), ()))
NT = (((1,), (1,)), ((), ()))
TN = (((0,), (0,)), ((), ()))


def dot(a, b, dims=NN):
    return lax.dot_general(a, b, dims, preferred_element_type=F32)


def inverse_rms(values):
    return lax.rsqrt(jnp.mean(values * values, axis=-1, keepdims=True) + EPS)


def norm_back(values, inverse, gain, upstream):
    scaled = gain * upstream
    inner = jnp.mean(scaled * values, axis=-1, keepdims=True)
    return inverse * scaled - values * (inverse * inverse * inverse * inner)


def cell_major():
    to = lax.broadcasted_iota(jnp.int32, (ROWS, ROWS), 0)
    at = lax.broadcasted_iota(jnp.int32, (ROWS, ROWS), 1)
    return (at == (to % 32) * 8 + to // 32).astype(F32).astype(BF16)


def member_major():
    to = lax.broadcasted_iota(jnp.int32, (ROWS, ROWS), 0)
    at = lax.broadcasted_iota(jnp.int32, (ROWS, ROWS), 1)
    return (at == (to % 8) * 32 + to // 8).astype(F32).astype(BF16)


def head_split(rows):
    first = lax.broadcasted_iota(jnp.int32, rows.shape, 1) < 64
    zero = jnp.zeros_like(rows)
    return jnp.concatenate([jnp.where(first, rows, zero), jnp.where(first, zero, rows)], axis=0)


def head_join(stacked):
    first = lax.broadcasted_iota(jnp.int32, (BLOCK, 128), 1) < 64
    return jnp.where(first, stacked[:BLOCK], stacked[BLOCK:])


def own_group(width, size):
    return (lax.broadcasted_iota(jnp.int32, (size, width), 1) % BLOCK) // size


def compact(full, size):
    group = own_group(full.shape[1], size)
    kept = full[:size]
    for g in range(1, BLOCK // size):
        kept = jnp.where(group == g, full[g * size : (g + 1) * size], kept)
    return kept


def expand(kept, size):
    group = own_group(kept.shape[1], size)
    zero = jnp.zeros_like(kept)
    return jnp.concatenate(
        [jnp.where(group == g, kept, zero) for g in range(BLOCK // size)], axis=0
    ).astype(BF16)


def softmax_keys(scores):
    raised = jnp.exp(scores - jnp.max(scores, axis=0, keepdims=True))
    return raised * (1.0 / jnp.sum(raised, axis=0, keepdims=True))


def blocks():
    return [
        (slice(b * BLOCK, (b + 1) * BLOCK), slice(p * 128, (p + 1) * 128))
        for b in range(ROWS // BLOCK)
        for p in range(PAIRS)
    ]


def attention_probs(q_split, k_ref, size):
    scores = [dot(k_ref[at], q, NT) for at, q in zip(blocks(), q_split)]
    scores = [compact(s, size) * SCALE for s in scores]
    return [softmax_keys(s) for s in scores]


def attention_backward(probs, q_split, k_ref, v_ref, do_split, dq_ref, dk_ref, dv_ref, size):
    grads = [dot(v_ref[at], do, NT) for at, do in zip(blocks(), do_split)]
    grads = [compact(g, size) for g in grads]
    wide = [expand(p, size) for p in probs]
    ds = [
        expand(p * (g - jnp.sum(p * g, axis=0, keepdims=True)) * SCALE, size)
        for p, g in zip(probs, grads)
    ]
    for at, p, do in zip(blocks(), wide, do_split):
        dv_ref[at] = dot(p, do).astype(BF16)
    for at, d, q in zip(blocks(), ds, q_split):
        dk_ref[at] = dot(d, q).astype(BF16)
    for at, d in zip(blocks(), ds):
        dq_ref[at] = head_join(dot(d, k_ref[at], TN)).astype(BF16)


def spread_kernel(state_hbm, cot_hbm, obs_hbm, out_ref, state_ref, cot_ref, obs_ref, sems):
    copies = [
        pltpu.make_async_copy(src, dst, sems.at[i])
        for i, (src, dst) in enumerate(
            ((obs_hbm, obs_ref), (state_hbm, state_ref), (cot_hbm, cot_ref))
        )
    ]
    for copy in copies:
        copy.start()
    for copy in copies:
        copy.wait()
    obs = obs_ref[...].astype(F32)
    eye = lax.broadcasted_iota(jnp.int32, (16, 16, 16), 1) == lax.broadcasted_iota(
        jnp.int32, (16, 16, 16), 2
    )
    weight = jnp.sum(jnp.where(eye, obs[:, None, :], 0.0), axis=-1, keepdims=True)
    dy = cot_ref[...].astype(F32) * weight
    parts = []
    for values in (state_ref[...].astype(F32), dy):
        inner = values[:, 4:12]
        west = values[:, 0:4].reshape(8, 2, 4, D)
        east = values[:, 12:16].reshape(8, 2, 4, D)
        parts.append(
            [
                jnp.concatenate([west[:, 0], west[:, 1]], axis=1),
                inner,
                jnp.concatenate([east[:, 0], east[:, 1]], axis=1),
            ]
        )
    sent = [jnp.concatenate([a, b], axis=1).astype(BF16) for a, b in zip(parts[0], parts[1])]
    sent = jnp.concatenate(sent, axis=0)
    for block, at in enumerate(places()):
        out_ref[at] = sent[block]


def gather_kernel(in_ref, out_ref):
    values = jnp.stack([in_ref[at] for at in places()]).astype(F32)
    west, east = values[0:8], values[24:32]
    inner = values[8:24].reshape(8, 2, 8, D)
    rows = [
        jnp.concatenate([west[:, 4 * i : 4 * i + 4], inner[:, i], east[:, 4 * i : 4 * i + 4]], axis=1)
        for i in range(2)
    ]
    out_ref[...] = jnp.stack(rows, axis=1).reshape(16, 16, D).astype(BF16)


def member_forward_kernel(
    in_ref, gain_ref, w_ref, out_ref, state_ref, q_ref, k_ref, v_ref, probs_ref, attended_ref
):
    values = in_ref[...].astype(F32)
    state = dot(cell_major(), values[:, :8].reshape(ROWS, D).astype(BF16))
    state_ref[...] = state.astype(BF16)
    normed = (state * inverse_rms(state) * gain_ref[...]).astype(BF16)
    q_ref[...] = dot(normed, w_ref[0]).astype(BF16)
    k_ref[...] = dot(normed, w_ref[1]).astype(BF16)
    v_ref[...] = dot(normed, w_ref[2]).astype(BF16)
    probs = attention_probs([head_split(q_ref[at]) for at in blocks()], k_ref, 32)
    for i, p in enumerate(probs):
        probs_ref[i] = p
    for at, p in zip(blocks(), probs):
        attended_ref[at] = head_join(dot(expand(p, 32), v_ref[at], TN)).astype(BF16)
    hidden = (state + dot(attended_ref[...], w_ref[3])).astype(BF16)
    hidden = dot(member_major(), hidden).reshape(32, 8, D)
    out_ref[...] = jnp.concatenate([hidden, values[:, 8:]], axis=1).astype(BF16).reshape(8, 4, 16, D)


def window_kernel(
    in_ref, gain_ref, w_ref, out_ref, q_ref, k_ref, v_ref, do_ref, dq_ref, dk_ref, dv_ref
):
    values = in_ref[...].astype(F32)
    hidden = jnp.concatenate([values[:, m, :8].reshape(64, D) for m in range(4)], axis=0)
    dy = jnp.concatenate([values[:, m, 8:].reshape(64, D) for m in range(4)], axis=0)
    inverse = inverse_rms(hidden)
    normed = (hidden * inverse * gain_ref[...]).astype(BF16)
    q_ref[...] = dot(normed, w_ref[0]).astype(BF16)
    k_ref[...] = dot(normed, w_ref[1]).astype(BF16)
    v_ref[...] = dot(normed, w_ref[2]).astype(BF16)
    do_ref[...] = dot(dy.astype(BF16), w_ref[3], NT).astype(BF16)
    q_split = [head_split(q_ref[at]) for at in blocks()]
    do_split = [head_split(do_ref[at]) for at in blocks()]
    probs = attention_probs(q_split, k_ref, 64)
    attention_backward(probs, q_split, k_ref, v_ref, do_split, dq_ref, dk_ref, dv_ref, 64)
    upstream = (
        dot(dq_ref[...], w_ref[0], NT) + dot(dk_ref[...], w_ref[1], NT) + dot(dv_ref[...], w_ref[2], NT)
    )
    grad = dy + norm_back(hidden, inverse, gain_ref[...], upstream)
    for m in range(4):
        out_ref[:, m] = grad[m * 64 : (m + 1) * 64].reshape(8, 8, D).astype(BF16)


def member_backward_kernel(
    in_ref, state_ref, q_ref, k_ref, v_ref, probs_ref, gain_ref, w_ref, out_ref, do_ref, dq_ref, dk_ref, dv_ref
):
    values = in_ref[...].astype(F32).reshape(ROWS, D).astype(BF16)
    hidden_grad = dot(cell_major(), values)
    do_ref[...] = dot(hidden_grad.astype(BF16), w_ref[3], NT).astype(BF16)
    q_split = [head_split(q_ref[at]) for at in blocks()]
    do_split = [head_split(do_ref[at]) for at in blocks()]
    probs = [probs_ref[i] for i in range(len(q_split))]
    attention_backward(probs, q_split, k_ref, v_ref, do_split, dq_ref, dk_ref, dv_ref, 32)
    upstream = (
        dot(dq_ref[...], w_ref[0], NT) + dot(dk_ref[...], w_ref[1], NT) + dot(dv_ref[...], w_ref[2], NT)
    )
    state = state_ref[...].astype(F32)
    grad = (hidden_grad + norm_back(state, inverse_rms(state), gain_ref[...], upstream)).astype(BF16)
    out_ref[...] = dot(member_major(), grad).astype(BF16).reshape(32, 8, D)


def call(kernel, outs, scratch=()):
    return pl.pallas_call(
        kernel,
        out_shape=outs,
        scratch_shapes=[pltpu.VMEM(s, t) for s, t in scratch],
        compiler_params=pltpu.CompilerParams(vmem_limit_bytes=32 * 1024 * 1024),
    )


def shape(dims, dtype=BF16):
    return jax.ShapeDtypeStruct(dims, dtype)


def holders(turned):
    def at(y, z):
        return y * 4 + z

    inner, outer = ((0, 1), (2, 3)) if turned else ((2, 3), (0, 1))
    low = [at(half + y, z) for half in (0, 4) for y in outer for z in (0, 1)]
    high = [at(half + y, z) for half in (0, 4) for y in outer for z in (3, 2)]
    within = [at(half + y, z) for half in (0, 4) for y in inner for z in range(4)]
    return high + within + low if turned else low + within + high


def is_turned(patch):
    return patch % 2 == 1, patch % 8 != 7


def member_order():
    order = []
    for i in range(32):
        y = (i >> 1 & 1) * 4 + (i >> 2 & 1) * 2 + (i >> 3 & 1)
        z = (i & 1) * 2 + (i >> 4 & 1)
        order.append(y * 4 + (z + y) % 4)
    return order


def places():
    order = member_order()
    odd, near = is_turned(lax.axis_index("patch"))
    turned = jnp.logical_and(odd, near)
    return [
        jnp.where(turned, order.index(there), order.index(here))
        for here, there in zip(holders(False), holders(True))
    ]


def groups(patches):
    order = member_order()
    cells = [[m * patches + p for m in order] for p in range(patches)]
    held = [[m * patches + p for m in holders(all(is_turned(p)))] for p in range(patches)]
    windows = []
    for p in range(patches):
        here, east = held[p], held[(p + 1) % patches]
        windows += [here[8:16], here[16:24]]
        windows += [here[24:28] + east[0:4], here[28:32] + east[4:8]]
    return cells, windows


def exchange(array, parties):
    return lax.all_to_all(
        array, ("member", "patch"), 0, 0, axis_index_groups=parties, tiled=True
    )


def body(
    state_field, cotangent, obs_count, member_gain, spatial_gain, member_weights, spatial_weights
):
    cells, windows = groups(lax.axis_size("patch"))
    member_gain, spatial_gain = member_gain.reshape(1, D), spatial_gain.reshape(1, D)
    rows = (ROWS, D)
    sent = pl.pallas_call(
        spread_kernel,
        out_shape=shape((32, 16, D)),
        in_specs=[pl.BlockSpec(memory_space=pltpu.HBM)] * 3,
        scratch_shapes=[
            pltpu.VMEM((16, 16, D), BF16),
            pltpu.VMEM((16, 16, D), BF16),
            pltpu.VMEM((16, 16), jnp.int32),
            pltpu.SemaphoreType.DMA((3,)),
        ],
    )(state_field.reshape(16, 16, D), cotangent.reshape(16, 16, D), obs_count)
    at_cells = exchange(sent, cells)
    hidden, state, q, k, v, probs = call(
        member_forward_kernel,
        [shape((8, 4, 16, D))] + [shape(rows)] * 4 + [shape((8, 32, 256), F32)],
        [(rows, BF16)],
    )(at_cells, member_gain, member_weights)
    at_windows = exchange(hidden, windows)
    grads = call(window_kernel, shape((8, 4, 8, D)), [(rows, BF16)] * 7)(
        at_windows, spatial_gain, spatial_weights
    )
    back_at_cells = exchange(grads, windows)
    field = call(member_backward_kernel, shape((32, 8, D)), [(rows, BF16)] * 4)(
        back_at_cells, state, q, k, v, probs, member_gain, member_weights
    )
    returned = exchange(field, cells)
    out = call(gather_kernel, shape((16, 16, D)))(returned)
    return out.reshape(1, 16, 16, D)


def solution(mesh):
    placed = (
        P("member", None, "patch", None),
        P("member", None, "patch", None),
        P(None, "patch"),
        P(),
        P(),
        P(),
        P(),
    )
    return jax.shard_map(
        body,
        mesh=mesh,
        in_specs=placed,
        out_specs=P("member", None, "patch", None),
        check_vma=False,
    )
```

```python
import jax
import jax.numpy as jnp
from jax import lax
from jax.experimental import pallas as pl
from jax.experimental.pallas import tpu as pltpu
from jax.sharding import PartitionSpec as P

F32 = jnp.float32
BF16 = jnp.bfloat16
D = 512
PAIRS = 4
SCALE = 64 ** (-0.5)
EPS = 1e-6
ROWS = 256
BLOCK = 128

NN = (((1,), (0,)), ((), ()))
NT = (((1,), (1,)), ((), ()))
TN = (((0,), (0,)), ((), ()))


def dot(a, b, dims=NN):
    return lax.dot_general(a, b, dims, preferred_element_type=F32)


def inverse_rms(values):
    return lax.rsqrt(jnp.mean(values * values, axis=-1, keepdims=True) + EPS)


def norm_back(values, inverse, gain, upstream):
    scaled = gain * upstream
    inner = jnp.mean(scaled * values, axis=-1, keepdims=True)
    return inverse * scaled - values * (inverse * inverse * inverse * inner)


def cell_major():
    to = lax.broadcasted_iota(jnp.int32, (ROWS, ROWS), 0)
    at = lax.broadcasted_iota(jnp.int32, (ROWS, ROWS), 1)
    return (at == (to % 32) * 8 + to // 32).astype(F32).astype(BF16)


def member_major():
    to = lax.broadcasted_iota(jnp.int32, (ROWS, ROWS), 0)
    at = lax.broadcasted_iota(jnp.int32, (ROWS, ROWS), 1)
    return (at == (to % 8) * 32 + to // 8).astype(F32).astype(BF16)


def head_split(rows):
    first = lax.broadcasted_iota(jnp.int32, rows.shape, 1) < 64
    zero = jnp.zeros_like(rows)
    return jnp.concatenate([jnp.where(first, rows, zero), jnp.where(first, zero, rows)], axis=0)


def head_join(stacked):
    first = lax.broadcasted_iota(jnp.int32, (BLOCK, 128), 1) < 64
    return jnp.where(first, stacked[:BLOCK], stacked[BLOCK:])


def own_group(width, size):
    return (lax.broadcasted_iota(jnp.int32, (size, width), 1) % BLOCK) // size


def compact(full, size):
    group = own_group(full.shape[1], size)
    kept = full[:size]
    for g in range(1, BLOCK // size):
        kept = jnp.where(group == g, full[g * size : (g + 1) * size], kept)
    return kept


def expand(kept, size):
    group = own_group(kept.shape[1], size)
    zero = jnp.zeros_like(kept)
    return jnp.concatenate(
        [jnp.where(group == g, kept, zero) for g in range(BLOCK // size)], axis=0
    ).astype(BF16)


def softmax_keys(scores):
    raised = jnp.exp(scores - jnp.max(scores, axis=0, keepdims=True))
    return raised * (1.0 / jnp.sum(raised, axis=0, keepdims=True))


def blocks():
    return [
        (slice(b * BLOCK, (b + 1) * BLOCK), slice(p * 128, (p + 1) * 128))
        for b in range(ROWS // BLOCK)
        for p in range(PAIRS)
    ]


def attention_probs(q_split, k_ref, size):
    scores = [dot(k_ref[at], q, NT) for at, q in zip(blocks(), q_split)]
    scores = [compact(s, size) * SCALE for s in scores]
    return [softmax_keys(s) for s in scores]


def attention_backward(probs, q_split, k_ref, v_ref, do_split, dq_ref, dk_ref, dv_ref, size):
    grads = [dot(v_ref[at], do, NT) for at, do in zip(blocks(), do_split)]
    grads = [compact(g, size) for g in grads]
    wide = [expand(p, size) for p in probs]
    ds = [
        expand(p * (g - jnp.sum(p * g, axis=0, keepdims=True)) * SCALE, size)
        for p, g in zip(probs, grads)
    ]
    for at, p, do in zip(blocks(), wide, do_split):
        dv_ref[at] = dot(p, do).astype(BF16)
    for at, d, q in zip(blocks(), ds, q_split):
        dk_ref[at] = dot(d, q).astype(BF16)
    for at, d in zip(blocks(), ds):
        dq_ref[at] = head_join(dot(d, k_ref[at], TN)).astype(BF16)


def spread_kernel(state_hbm, cot_hbm, obs_hbm, out_ref, state_ref, cot_ref, obs_ref, sems):
    copies = [
        pltpu.make_async_copy(src, dst, sems.at[i])
        for i, (src, dst) in enumerate(
            ((obs_hbm, obs_ref), (state_hbm, state_ref), (cot_hbm, cot_ref))
        )
    ]
    for copy in copies:
        copy.start()
    for copy in copies:
        copy.wait()
    obs = obs_ref[...].astype(F32)
    eye = lax.broadcasted_iota(jnp.int32, (16, 16, 16), 1) == lax.broadcasted_iota(
        jnp.int32, (16, 16, 16), 2
    )
    weight = jnp.sum(jnp.where(eye, obs[:, None, :], 0.0), axis=-1, keepdims=True)
    dy = cot_ref[...].astype(F32) * weight
    parts = []
    for values in (state_ref[...].astype(F32), dy):
        inner = values[:, 4:12]
        west = values[:, 0:4].reshape(8, 2, 4, D)
        east = values[:, 12:16].reshape(8, 2, 4, D)
        parts.append(
            [
                jnp.concatenate([west[:, 0], west[:, 1]], axis=1),
                inner,
                jnp.concatenate([east[:, 0], east[:, 1]], axis=1),
            ]
        )
    sent = [jnp.concatenate([a, b], axis=1).astype(BF16) for a, b in zip(parts[0], parts[1])]
    sent = jnp.concatenate(sent, axis=0)
    for block, at in enumerate(places()):
        out_ref[at] = sent[block]


def gather_kernel(in_ref, out_ref):
    values = jnp.stack([in_ref[at] for at in places()]).astype(F32)
    west, east = values[0:8], values[24:32]
    inner = values[8:24].reshape(8, 2, 8, D)
    rows = [
        jnp.concatenate([west[:, 4 * i : 4 * i + 4], inner[:, i], east[:, 4 * i : 4 * i + 4]], axis=1)
        for i in range(2)
    ]
    out_ref[...] = jnp.stack(rows, axis=1).reshape(16, 16, D).astype(BF16)


def member_forward_kernel(
    in_ref, gain_ref, w_ref, out_ref, state_ref, q_ref, k_ref, v_ref, probs_ref, attended_ref
):
    values = in_ref[...].astype(F32)
    state = dot(cell_major(), values[:, :8].reshape(ROWS, D).astype(BF16))
    state_ref[...] = state.astype(BF16)
    normed = (state * inverse_rms(state) * gain_ref[...]).astype(BF16)
    q_ref[...] = dot(normed, w_ref[0]).astype(BF16)
    k_ref[...] = dot(normed, w_ref[1]).astype(BF16)
    v_ref[...] = dot(normed, w_ref[2]).astype(BF16)
    probs = attention_probs([head_split(q_ref[at]) for at in blocks()], k_ref, 32)
    for i, p in enumerate(probs):
        probs_ref[i] = p
    for at, p in zip(blocks(), probs):
        attended_ref[at] = head_join(dot(expand(p, 32), v_ref[at], TN)).astype(BF16)
    hidden = (state + dot(attended_ref[...], w_ref[3])).astype(BF16)
    hidden = dot(member_major(), hidden).reshape(32, 8, D)
    out_ref[...] = jnp.concatenate([hidden, values[:, 8:]], axis=1).astype(BF16).reshape(8, 4, 16, D)


def window_kernel(
    in_ref, gain_ref, w_ref, out_ref, q_ref, k_ref, v_ref, do_ref, dq_ref, dk_ref, dv_ref
):
    values = in_ref[...].astype(F32)
    hidden = jnp.concatenate([values[:, m, :8].reshape(64, D) for m in range(4)], axis=0)
    dy = jnp.concatenate([values[:, m, 8:].reshape(64, D) for m in range(4)], axis=0)
    inverse = inverse_rms(hidden)
    normed = (hidden * inverse * gain_ref[...]).astype(BF16)
    q_ref[...] = dot(normed, w_ref[0]).astype(BF16)
    k_ref[...] = dot(normed, w_ref[1]).astype(BF16)
    v_ref[...] = dot(normed, w_ref[2]).astype(BF16)
    do_ref[...] = dot(dy.astype(BF16), w_ref[3], NT).astype(BF16)
    q_split = [head_split(q_ref[at]) for at in blocks()]
    do_split = [head_split(do_ref[at]) for at in blocks()]
    probs = attention_probs(q_split, k_ref, 64)
    attention_backward(probs, q_split, k_ref, v_ref, do_split, dq_ref, dk_ref, dv_ref, 64)
    upstream = (
        dot(dq_ref[...], w_ref[0], NT) + dot(dk_ref[...], w_ref[1], NT) + dot(dv_ref[...], w_ref[2], NT)
    )
    grad = dy + norm_back(hidden, inverse, gain_ref[...], upstream)
    for m in range(4):
        out_ref[:, m] = grad[m * 64 : (m + 1) * 64].reshape(8, 8, D).astype(BF16)


def member_backward_kernel(
    in_ref, state_ref, q_ref, k_ref, v_ref, probs_ref, gain_ref, w_ref, out_ref, do_ref, dq_ref, dk_ref, dv_ref
):
    values = in_ref[...].astype(F32).reshape(ROWS, D).astype(BF16)
    hidden_grad = dot(cell_major(), values)
    do_ref[...] = dot(hidden_grad.astype(BF16), w_ref[3], NT).astype(BF16)
    q_split = [head_split(q_ref[at]) for at in blocks()]
    do_split = [head_split(do_ref[at]) for at in blocks()]
    probs = [probs_ref[i] for i in range(len(q_split))]
    attention_backward(probs, q_split, k_ref, v_ref, do_split, dq_ref, dk_ref, dv_ref, 32)
    upstream = (
        dot(dq_ref[...], w_ref[0], NT) + dot(dk_ref[...], w_ref[1], NT) + dot(dv_ref[...], w_ref[2], NT)
    )
    state = state_ref[...].astype(F32)
    grad = (hidden_grad + norm_back(state, inverse_rms(state), gain_ref[...], upstream)).astype(BF16)
    out_ref[...] = dot(member_major(), grad).astype(BF16).reshape(32, 8, D)


def call(kernel, outs, scratch=()):
    return pl.pallas_call(
        kernel,
        out_shape=outs,
        scratch_shapes=[pltpu.VMEM(s, t) for s, t in scratch],
        compiler_params=pltpu.CompilerParams(vmem_limit_bytes=32 * 1024 * 1024),
    )


def shape(dims, dtype=BF16):
    return jax.ShapeDtypeStruct(dims, dtype)


def holders(turned):
    def at(y, z):
        return y * 4 + z

    inner, outer = ((0, 1), (2, 3)) if turned else ((2, 3), (0, 1))
    low = [at(half + y, z) for half in (0, 4) for y in outer for z in (0, 1)]
    high = [at(half + y, z) for half in (0, 4) for y in outer for z in (3, 2)]
    within = [at(half + y, z) for half in (0, 4) for y in inner for z in range(4)]
    return high + within + low if turned else low + within + high


def is_turned(patch):
    return patch % 2 == 1, patch % 8 != 7


def member_order():
    return [y * 4 + (z + y) % 4 for z in range(4) for y in range(8)]


def places():
    order = member_order()
    odd, near = is_turned(lax.axis_index("patch"))
    turned = jnp.logical_and(odd, near)
    return [
        jnp.where(turned, order.index(there), order.index(here))
        for here, there in zip(holders(False), holders(True))
    ]


def groups(patches):
    order = member_order()
    cells = [[m * patches + p for m in order] for p in range(patches)]
    held = [[m * patches + p for m in holders(all(is_turned(p)))] for p in range(patches)]
    windows = []
    for p in range(patches):
        here, east = held[p], held[(p + 1) % patches]
        windows += [here[8:16], here[16:24]]
        windows += [here[24:28] + east[0:4], here[28:32] + east[4:8]]
    return cells, windows


def exchange(array, parties):
    return lax.all_to_all(
        array, ("member", "patch"), 0, 0, axis_index_groups=parties, tiled=True
    )


def body(
    state_field, cotangent, obs_count, member_gain, spatial_gain, member_weights, spatial_weights
):
    cells, windows = groups(lax.axis_size("patch"))
    member_gain, spatial_gain = member_gain.reshape(1, D), spatial_gain.reshape(1, D)
    rows = (ROWS, D)
    sent = pl.pallas_call(
        spread_kernel,
        out_shape=shape((32, 16, D)),
        in_specs=[pl.BlockSpec(memory_space=pltpu.HBM)] * 3,
        scratch_shapes=[
            pltpu.VMEM((16, 16, D), BF16),
            pltpu.VMEM((16, 16, D), BF16),
            pltpu.VMEM((16, 16), jnp.int32),
            pltpu.SemaphoreType.DMA((3,)),
        ],
    )(state_field.reshape(16, 16, D), cotangent.reshape(16, 16, D), obs_count)
    at_cells = exchange(sent, cells)
    hidden, state, q, k, v, probs = call(
        member_forward_kernel,
        [shape((8, 4, 16, D))] + [shape(rows)] * 4 + [shape((8, 32, 256), F32)],
        [(rows, BF16)],
    )(at_cells, member_gain, member_weights)
    at_windows = exchange(hidden, windows)
    grads = call(window_kernel, shape((8, 4, 8, D)), [(rows, BF16)] * 7)(
        at_windows, spatial_gain, spatial_weights
    )
    back_at_cells = exchange(grads, windows)
    field = call(member_backward_kernel, shape((32, 8, D)), [(rows, BF16)] * 4)(
        back_at_cells, state, q, k, v, probs, member_gain, member_weights
    )
    returned = exchange(field, cells)
    out = call(gather_kernel, shape((16, 16, D)))(returned)
    return out.reshape(1, 16, 16, D)


def solution(mesh):
    placed = (
        P("member", None, "patch", None),
        P("member", None, "patch", None),
        P(None, "patch"),
        P(),
        P(),
        P(),
        P(),
    )
    return jax.shard_map(
        body,
        mesh=mesh,
        in_specs=placed,
        out_specs=P("member", None, "patch", None),
        check_vma=False,
    )
```

```python
import jax
import jax.numpy as jnp
from jax import lax
from jax.experimental import pallas as pl
from jax.experimental.pallas import tpu as pltpu
from jax.sharding import PartitionSpec as P

F32 = jnp.float32
BF16 = jnp.bfloat16
D = 512
PAIRS = 4
SCALE = 64 ** (-0.5)
EPS = 1e-6
ROWS = 256
BLOCK = 128

NN = (((1,), (0,)), ((), ()))
NT = (((1,), (1,)), ((), ()))
TN = (((0,), (0,)), ((), ()))


def dot(a, b, dims=NN):
    return lax.dot_general(a, b, dims, preferred_element_type=F32)


def inverse_rms(values):
    return lax.rsqrt(jnp.mean(values * values, axis=-1, keepdims=True) + EPS)


def norm_back(values, inverse, gain, upstream):
    scaled = gain * upstream
    inner = jnp.mean(scaled * values, axis=-1, keepdims=True)
    return inverse * scaled - values * (inverse * inverse * inverse * inner)


def cell_major():
    to = lax.broadcasted_iota(jnp.int32, (ROWS, ROWS), 0)
    at = lax.broadcasted_iota(jnp.int32, (ROWS, ROWS), 1)
    return (at == (to % 32) * 8 + to // 32).astype(F32).astype(BF16)


def member_major():
    to = lax.broadcasted_iota(jnp.int32, (ROWS, ROWS), 0)
    at = lax.broadcasted_iota(jnp.int32, (ROWS, ROWS), 1)
    return (at == (to % 8) * 32 + to // 8).astype(F32).astype(BF16)


def head_split(rows):
    first = lax.broadcasted_iota(jnp.int32, rows.shape, 1) < 64
    zero = jnp.zeros_like(rows)
    return jnp.concatenate([jnp.where(first, rows, zero), jnp.where(first, zero, rows)], axis=0)


def head_join(stacked):
    first = lax.broadcasted_iota(jnp.int32, (BLOCK, 128), 1) < 64
    return jnp.where(first, stacked[:BLOCK], stacked[BLOCK:])


def own_group(width, size):
    return (lax.broadcasted_iota(jnp.int32, (size, width), 1) % BLOCK) // size


def compact(full, size):
    group = own_group(full.shape[1], size)
    kept = full[:size]
    for g in range(1, BLOCK // size):
        kept = jnp.where(group == g, full[g * size : (g + 1) * size], kept)
    return kept


def expand(kept, size):
    group = own_group(kept.shape[1], size)
    zero = jnp.zeros_like(kept)
    return jnp.concatenate(
        [jnp.where(group == g, kept, zero) for g in range(BLOCK // size)], axis=0
    ).astype(BF16)


def softmax_keys(scores):
    raised = jnp.exp(scores - jnp.max(scores, axis=0, keepdims=True))
    return raised * (1.0 / jnp.sum(raised, axis=0, keepdims=True))


def blocks():
    return [
        (slice(b * BLOCK, (b + 1) * BLOCK), slice(p * 128, (p + 1) * 128))
        for b in range(ROWS // BLOCK)
        for p in range(PAIRS)
    ]


def attention_probs(q_split, k_ref, size):
    scores = [dot(k_ref[at], q, NT) for at, q in zip(blocks(), q_split)]
    scores = [compact(s, size) * SCALE for s in scores]
    return [softmax_keys(s) for s in scores]


def attention_backward(probs, q_split, k_ref, v_ref, do_split, dq_ref, dk_ref, dv_ref, size):
    grads = [dot(v_ref[at], do, NT) for at, do in zip(blocks(), do_split)]
    grads = [compact(g, size) for g in grads]
    wide = [expand(p, size) for p in probs]
    ds = [
        expand(p * (g - jnp.sum(p * g, axis=0, keepdims=True)) * SCALE, size)
        for p, g in zip(probs, grads)
    ]
    for at, p, do in zip(blocks(), wide, do_split):
        dv_ref[at] = dot(p, do).astype(BF16)
    for at, d, q in zip(blocks(), ds, q_split):
        dk_ref[at] = dot(d, q).astype(BF16)
    for at, d in zip(blocks(), ds):
        dq_ref[at] = head_join(dot(d, k_ref[at], TN)).astype(BF16)


def spread_kernel(state_hbm, cot_hbm, obs_hbm, out_ref, state_ref, cot_ref, obs_ref, sems):
    copies = [
        pltpu.make_async_copy(src, dst, sems.at[i])
        for i, (src, dst) in enumerate(
            ((obs_hbm, obs_ref), (state_hbm, state_ref), (cot_hbm, cot_ref))
        )
    ]
    for copy in copies:
        copy.start()
    for copy in copies:
        copy.wait()
    obs = obs_ref[...].astype(F32)
    eye = lax.broadcasted_iota(jnp.int32, (16, 16, 16), 1) == lax.broadcasted_iota(
        jnp.int32, (16, 16, 16), 2
    )
    weight = jnp.sum(jnp.where(eye, obs[:, None, :], 0.0), axis=-1, keepdims=True)
    dy = cot_ref[...].astype(F32) * weight
    parts = []
    for values in (state_ref[...].astype(F32), dy):
        inner = values[:, 4:12]
        west = values[:, 0:4].reshape(8, 2, 4, D)
        east = values[:, 12:16].reshape(8, 2, 4, D)
        parts.append(
            [
                jnp.concatenate([west[:, 0], west[:, 1]], axis=1),
                inner,
                jnp.concatenate([east[:, 0], east[:, 1]], axis=1),
            ]
        )
    sent = [jnp.concatenate([a, b], axis=1).astype(BF16) for a, b in zip(parts[0], parts[1])]
    sent = jnp.concatenate(sent, axis=0)
    for block, at in enumerate(places(member_order())):
        out_ref[at] = sent[block]


def gather_kernel(in_ref, out_ref):
    values = jnp.stack([in_ref[at] for at in places(return_order())]).astype(F32)
    west, east = values[0:8], values[24:32]
    inner = values[8:24].reshape(8, 2, 8, D)
    rows = [
        jnp.concatenate([west[:, 4 * i : 4 * i + 4], inner[:, i], east[:, 4 * i : 4 * i + 4]], axis=1)
        for i in range(2)
    ]
    out_ref[...] = jnp.stack(rows, axis=1).reshape(16, 16, D).astype(BF16)


def member_forward_kernel(
    in_ref, gain_ref, w_ref, out_ref, state_ref, q_ref, k_ref, v_ref, probs_ref, attended_ref
):
    values = in_ref[...].astype(F32)
    state = dot(cell_major(), values[:, :8].reshape(ROWS, D).astype(BF16))
    state_ref[...] = state.astype(BF16)
    normed = (state * inverse_rms(state) * gain_ref[...]).astype(BF16)
    q_ref[...] = dot(normed, w_ref[0]).astype(BF16)
    k_ref[...] = dot(normed, w_ref[1]).astype(BF16)
    v_ref[...] = dot(normed, w_ref[2]).astype(BF16)
    probs = attention_probs([head_split(q_ref[at]) for at in blocks()], k_ref, 32)
    for i, p in enumerate(probs):
        probs_ref[i] = p
    for at, p in zip(blocks(), probs):
        attended_ref[at] = head_join(dot(expand(p, 32), v_ref[at], TN)).astype(BF16)
    hidden = (state + dot(attended_ref[...], w_ref[3])).astype(BF16)
    hidden = dot(member_major(), hidden).reshape(32, 8, D)
    out_ref[...] = jnp.concatenate([hidden, values[:, 8:]], axis=1).astype(BF16).reshape(8, 4, 16, D)


def window_kernel(
    in_ref, gain_ref, w_ref, out_ref, q_ref, k_ref, v_ref, do_ref, dq_ref, dk_ref, dv_ref
):
    values = in_ref[...].astype(F32)
    hidden = jnp.concatenate([values[:, m, :8].reshape(64, D) for m in range(4)], axis=0)
    dy = jnp.concatenate([values[:, m, 8:].reshape(64, D) for m in range(4)], axis=0)
    inverse = inverse_rms(hidden)
    normed = (hidden * inverse * gain_ref[...]).astype(BF16)
    q_ref[...] = dot(normed, w_ref[0]).astype(BF16)
    k_ref[...] = dot(normed, w_ref[1]).astype(BF16)
    v_ref[...] = dot(normed, w_ref[2]).astype(BF16)
    do_ref[...] = dot(dy.astype(BF16), w_ref[3], NT).astype(BF16)
    q_split = [head_split(q_ref[at]) for at in blocks()]
    do_split = [head_split(do_ref[at]) for at in blocks()]
    probs = attention_probs(q_split, k_ref, 64)
    attention_backward(probs, q_split, k_ref, v_ref, do_split, dq_ref, dk_ref, dv_ref, 64)
    upstream = (
        dot(dq_ref[...], w_ref[0], NT) + dot(dk_ref[...], w_ref[1], NT) + dot(dv_ref[...], w_ref[2], NT)
    )
    grad = dy + norm_back(hidden, inverse, gain_ref[...], upstream)
    for m in range(4):
        out_ref[:, m] = grad[m * 64 : (m + 1) * 64].reshape(8, 8, D).astype(BF16)


def member_backward_kernel(
    in_ref, state_ref, q_ref, k_ref, v_ref, probs_ref, gain_ref, w_ref, out_ref, do_ref, dq_ref, dk_ref, dv_ref
):
    values = in_ref[...].astype(F32).reshape(ROWS, D).astype(BF16)
    hidden_grad = dot(cell_major(), values)
    do_ref[...] = dot(hidden_grad.astype(BF16), w_ref[3], NT).astype(BF16)
    q_split = [head_split(q_ref[at]) for at in blocks()]
    do_split = [head_split(do_ref[at]) for at in blocks()]
    probs = [probs_ref[i] for i in range(len(q_split))]
    attention_backward(probs, q_split, k_ref, v_ref, do_split, dq_ref, dk_ref, dv_ref, 32)
    upstream = (
        dot(dq_ref[...], w_ref[0], NT) + dot(dk_ref[...], w_ref[1], NT) + dot(dv_ref[...], w_ref[2], NT)
    )
    state = state_ref[...].astype(F32)
    grad = (hidden_grad + norm_back(state, inverse_rms(state), gain_ref[...], upstream)).astype(BF16)
    grad = dot(member_major(), grad).reshape(32, 8, D).astype(BF16)
    order = member_order()
    for k, m in enumerate(return_order()):
        out_ref[k] = grad[order.index(m)]


def call(kernel, outs, scratch=()):
    return pl.pallas_call(
        kernel,
        out_shape=outs,
        scratch_shapes=[pltpu.VMEM(s, t) for s, t in scratch],
        compiler_params=pltpu.CompilerParams(vmem_limit_bytes=32 * 1024 * 1024),
    )


def shape(dims, dtype=BF16):
    return jax.ShapeDtypeStruct(dims, dtype)


def holders(turned):
    def at(y, z):
        return y * 4 + z

    inner, outer = ((0, 1), (2, 3)) if turned else ((2, 3), (0, 1))
    low = [at(half + y, z) for half in (0, 4) for y in outer for z in (0, 1)]
    high = [at(half + y, z) for half in (0, 4) for y in outer for z in (3, 2)]
    within = [at(half + y, z) for half in (0, 4) for y in inner for z in range(4)]
    return high + within + low if turned else low + within + high


def is_turned(patch):
    return patch % 2 == 1, patch % 8 != 7


def member_order():
    return [15, 14, 27, 26, 11, 10, 31, 30, 19, 23, 18, 22, 0, 1, 4, 5, 16, 17, 20, 21, 3, 2, 7, 6, 8, 9, 12, 13, 24, 25, 28, 29]


def return_order():
    return [18, 19, 22, 23, 2, 3, 6, 7, 0, 4, 28, 1, 5, 29, 8, 24, 9, 25, 10, 11, 12, 13, 14, 15, 16, 17, 20, 21, 26, 27, 30, 31]


def places(order):
    odd, near = is_turned(lax.axis_index("patch"))
    turned = jnp.logical_and(odd, near)
    return [
        jnp.where(turned, order.index(there), order.index(here))
        for here, there in zip(holders(False), holders(True))
    ]


def groups(patches):
    cells, returns = (
        [[m * patches + p for m in order] for p in range(patches)]
        for order in (member_order(), return_order())
    )
    held = [[m * patches + p for m in holders(all(is_turned(p)))] for p in range(patches)]
    windows = []
    for p in range(patches):
        here, east = held[p], held[(p + 1) % patches]
        windows += [here[8:16], here[16:24]]
        windows += [here[24:28] + east[0:4], here[28:32] + east[4:8]]
    return cells, windows, returns


def exchange(array, parties):
    return lax.all_to_all(
        array, ("member", "patch"), 0, 0, axis_index_groups=parties, tiled=True
    )


def body(
    state_field, cotangent, obs_count, member_gain, spatial_gain, member_weights, spatial_weights
):
    cells, windows, returns = groups(lax.axis_size("patch"))
    member_gain, spatial_gain = member_gain.reshape(1, D), spatial_gain.reshape(1, D)
    rows = (ROWS, D)
    sent = pl.pallas_call(
        spread_kernel,
        out_shape=shape((32, 16, D)),
        in_specs=[pl.BlockSpec(memory_space=pltpu.HBM)] * 3,
        scratch_shapes=[
            pltpu.VMEM((16, 16, D), BF16),
            pltpu.VMEM((16, 16, D), BF16),
            pltpu.VMEM((16, 16), jnp.int32),
            pltpu.SemaphoreType.DMA((3,)),
        ],
    )(state_field.reshape(16, 16, D), cotangent.reshape(16, 16, D), obs_count)
    at_cells = exchange(sent, cells)
    hidden, state, q, k, v, probs = call(
        member_forward_kernel,
        [shape((8, 4, 16, D))] + [shape(rows)] * 4 + [shape((8, 32, 256), F32)],
        [(rows, BF16)],
    )(at_cells, member_gain, member_weights)
    at_windows = exchange(hidden, windows)
    grads = call(window_kernel, shape((8, 4, 8, D)), [(rows, BF16)] * 7)(
        at_windows, spatial_gain, spatial_weights
    )
    back_at_cells = exchange(grads, windows)
    field = call(member_backward_kernel, shape((32, 8, D)), [(rows, BF16)] * 4)(
        back_at_cells, state, q, k, v, probs, member_gain, member_weights
    )
    returned = exchange(field, returns)
    out = call(gather_kernel, shape((16, 16, D)))(returned)
    return out.reshape(1, 16, 16, D)


def solution(mesh):
    placed = (
        P("member", None, "patch", None),
        P("member", None, "patch", None),
        P(None, "patch"),
        P(),
        P(),
        P(),
        P(),
    )
    return jax.shard_map(
        body,
        mesh=mesh,
        in_specs=placed,
        out_specs=P("member", None, "patch", None),
        check_vma=False,
    )
```

```python
import jax
import jax.numpy as jnp
from jax import lax
from jax.experimental import pallas as pl
from jax.experimental.pallas import tpu as pltpu
from jax.sharding import PartitionSpec as P

F32 = jnp.float32
BF16 = jnp.bfloat16
D = 512
PAIRS = 4
SCALE = 64 ** (-0.5)
EPS = 1e-6
ROWS = 256
BLOCK = 128

NN = (((1,), (0,)), ((), ()))
NT = (((1,), (1,)), ((), ()))
TN = (((0,), (0,)), ((), ()))


def dot(a, b, dims=NN):
    return lax.dot_general(a, b, dims, preferred_element_type=F32)


def inverse_rms(values):
    return lax.rsqrt(jnp.mean(values * values, axis=-1, keepdims=True) + EPS)


def norm_back(values, inverse, gain, upstream):
    scaled = gain * upstream
    inner = jnp.mean(scaled * values, axis=-1, keepdims=True)
    return inverse * scaled - values * (inverse * inverse * inverse * inner)


def cell_major():
    to = lax.broadcasted_iota(jnp.int32, (ROWS, ROWS), 0)
    at = lax.broadcasted_iota(jnp.int32, (ROWS, ROWS), 1)
    return (at == (to % 32) * 8 + to // 32).astype(F32).astype(BF16)


def member_major():
    to = lax.broadcasted_iota(jnp.int32, (ROWS, ROWS), 0)
    at = lax.broadcasted_iota(jnp.int32, (ROWS, ROWS), 1)
    return (at == (to % 8) * 32 + to // 8).astype(F32).astype(BF16)


def head_split(rows):
    first = lax.broadcasted_iota(jnp.int32, rows.shape, 1) < 64
    zero = jnp.zeros_like(rows)
    return jnp.concatenate([jnp.where(first, rows, zero), jnp.where(first, zero, rows)], axis=0)


def head_join(stacked):
    first = lax.broadcasted_iota(jnp.int32, (BLOCK, 128), 1) < 64
    return jnp.where(first, stacked[:BLOCK], stacked[BLOCK:])


def own_group(width, size):
    return (lax.broadcasted_iota(jnp.int32, (size, width), 1) % BLOCK) // size


def compact(full, size):
    group = own_group(full.shape[1], size)
    kept = full[:size]
    for g in range(1, BLOCK // size):
        kept = jnp.where(group == g, full[g * size : (g + 1) * size], kept)
    return kept


def expand(kept, size):
    group = own_group(kept.shape[1], size)
    zero = jnp.zeros_like(kept)
    return jnp.concatenate(
        [jnp.where(group == g, kept, zero) for g in range(BLOCK // size)], axis=0
    ).astype(BF16)


def softmax_keys(scores):
    raised = jnp.exp(scores - jnp.max(scores, axis=0, keepdims=True))
    return raised * (1.0 / jnp.sum(raised, axis=0, keepdims=True))


def blocks():
    return [
        (slice(b * BLOCK, (b + 1) * BLOCK), slice(p * 128, (p + 1) * 128))
        for b in range(ROWS // BLOCK)
        for p in range(PAIRS)
    ]


def attention_probs(q_split, k_ref, size):
    scores = [dot(k_ref[at], q, NT) for at, q in zip(blocks(), q_split)]
    scores = [compact(s, size) * SCALE for s in scores]
    return [softmax_keys(s) for s in scores]


def attention_backward(probs, q_split, k_ref, v_ref, do_split, dq_ref, dk_ref, dv_ref, size):
    grads = [dot(v_ref[at], do, NT) for at, do in zip(blocks(), do_split)]
    grads = [compact(g, size) for g in grads]
    wide = [expand(p, size) for p in probs]
    ds = [
        expand(p * (g - jnp.sum(p * g, axis=0, keepdims=True)) * SCALE, size)
        for p, g in zip(probs, grads)
    ]
    for at, p, do in zip(blocks(), wide, do_split):
        dv_ref[at] = dot(p, do).astype(BF16)
    for at, d, q in zip(blocks(), ds, q_split):
        dk_ref[at] = dot(d, q).astype(BF16)
    for at, d in zip(blocks(), ds):
        dq_ref[at] = head_join(dot(d, k_ref[at], TN)).astype(BF16)


def spread_kernel(state_hbm, cot_hbm, obs_hbm, out_ref, state_ref, cot_ref, obs_ref, sems):
    copies = [
        pltpu.make_async_copy(src, dst, sems.at[i])
        for i, (src, dst) in enumerate(
            ((obs_hbm, obs_ref), (state_hbm, state_ref), (cot_hbm, cot_ref))
        )
    ]
    for copy in copies:
        copy.start()
    for copy in copies:
        copy.wait()
    obs = obs_ref[...].astype(F32)
    eye = lax.broadcasted_iota(jnp.int32, (16, 16, 16), 1) == lax.broadcasted_iota(
        jnp.int32, (16, 16, 16), 2
    )
    weight = jnp.sum(jnp.where(eye, obs[:, None, :], 0.0), axis=-1, keepdims=True)
    dy = cot_ref[...].astype(F32) * weight
    parts = []
    for values in (state_ref[...].astype(F32), dy):
        inner = values[:, 4:12]
        west = values[:, 0:4].reshape(8, 2, 4, D)
        east = values[:, 12:16].reshape(8, 2, 4, D)
        parts.append(
            [
                jnp.concatenate([west[:, 0], west[:, 1]], axis=1),
                inner,
                jnp.concatenate([east[:, 0], east[:, 1]], axis=1),
            ]
        )
    sent = [jnp.concatenate([a, b], axis=1).astype(BF16) for a, b in zip(parts[0], parts[1])]
    sent = jnp.concatenate(sent, axis=0)
    for block, at in enumerate(places(member_order())):
        out_ref[at] = sent[block]


def gather_kernel(in_ref, out_ref):
    values = jnp.stack([in_ref[at] for at in places(return_order())]).astype(F32)
    west, east = values[0:8], values[24:32]
    inner = values[8:24].reshape(8, 2, 8, D)
    rows = [
        jnp.concatenate([west[:, 4 * i : 4 * i + 4], inner[:, i], east[:, 4 * i : 4 * i + 4]], axis=1)
        for i in range(2)
    ]
    out_ref[...] = jnp.stack(rows, axis=1).reshape(16, 16, D).astype(BF16)


def member_forward_kernel(
    in_ref, gain_ref, w_ref, out_ref, state_ref, q_ref, k_ref, v_ref, probs_ref, attended_ref
):
    values = in_ref[...].astype(F32)
    state = dot(cell_major(), values[:, :8].reshape(ROWS, D).astype(BF16))
    state_ref[...] = state.astype(BF16)
    normed = (state * inverse_rms(state) * gain_ref[...]).astype(BF16)
    q_ref[...] = dot(normed, w_ref[0]).astype(BF16)
    k_ref[...] = dot(normed, w_ref[1]).astype(BF16)
    v_ref[...] = dot(normed, w_ref[2]).astype(BF16)
    probs = attention_probs([head_split(q_ref[at]) for at in blocks()], k_ref, 32)
    for i, p in enumerate(probs):
        probs_ref[i] = p
    for at, p in zip(blocks(), probs):
        attended_ref[at] = head_join(dot(expand(p, 32), v_ref[at], TN)).astype(BF16)
    hidden = (state + dot(attended_ref[...], w_ref[3])).astype(BF16)
    hidden = dot(member_major(), hidden).reshape(32, 8, D)
    out_ref[...] = jnp.concatenate([hidden, values[:, 8:]], axis=1).astype(BF16).reshape(8, 4, 16, D)


def window_kernel(
    in_ref, gain_ref, w_ref, out_ref, q_ref, k_ref, v_ref, do_ref, dq_ref, dk_ref, dv_ref
):
    values = in_ref[...].astype(F32)
    hidden = jnp.concatenate([values[:, m, :8].reshape(64, D) for m in range(4)], axis=0)
    dy = jnp.concatenate([values[:, m, 8:].reshape(64, D) for m in range(4)], axis=0)
    inverse = inverse_rms(hidden)
    normed = (hidden * inverse * gain_ref[...]).astype(BF16)
    q_ref[...] = dot(normed, w_ref[0]).astype(BF16)
    k_ref[...] = dot(normed, w_ref[1]).astype(BF16)
    v_ref[...] = dot(normed, w_ref[2]).astype(BF16)
    do_ref[...] = dot(dy.astype(BF16), w_ref[3], NT).astype(BF16)
    q_split = [head_split(q_ref[at]) for at in blocks()]
    do_split = [head_split(do_ref[at]) for at in blocks()]
    probs = attention_probs(q_split, k_ref, 64)
    attention_backward(probs, q_split, k_ref, v_ref, do_split, dq_ref, dk_ref, dv_ref, 64)
    upstream = (
        dot(dq_ref[...], w_ref[0], NT) + dot(dk_ref[...], w_ref[1], NT) + dot(dv_ref[...], w_ref[2], NT)
    )
    grad = dy + norm_back(hidden, inverse, gain_ref[...], upstream)
    for m in range(4):
        out_ref[:, m] = grad[m * 64 : (m + 1) * 64].reshape(8, 8, D).astype(BF16)


def member_backward_kernel(
    in_ref, state_ref, q_ref, k_ref, v_ref, probs_ref, gain_ref, w_ref, out_ref, do_ref, dq_ref, dk_ref, dv_ref
):
    values = in_ref[...].astype(F32).reshape(ROWS, D).astype(BF16)
    hidden_grad = dot(cell_major(), values)
    do_ref[...] = dot(hidden_grad.astype(BF16), w_ref[3], NT).astype(BF16)
    q_split = [head_split(q_ref[at]) for at in blocks()]
    do_split = [head_split(do_ref[at]) for at in blocks()]
    probs = [probs_ref[i] for i in range(len(q_split))]
    attention_backward(probs, q_split, k_ref, v_ref, do_split, dq_ref, dk_ref, dv_ref, 32)
    upstream = (
        dot(dq_ref[...], w_ref[0], NT) + dot(dk_ref[...], w_ref[1], NT) + dot(dv_ref[...], w_ref[2], NT)
    )
    state = state_ref[...].astype(F32)
    grad = (hidden_grad + norm_back(state, inverse_rms(state), gain_ref[...], upstream)).astype(BF16)
    grad = dot(member_major(), grad).reshape(32, 8, D).astype(BF16)
    order = member_order()
    for k, m in enumerate(return_order()):
        out_ref[k] = grad[order.index(m)]


def call(kernel, outs, scratch=()):
    return pl.pallas_call(
        kernel,
        out_shape=outs,
        scratch_shapes=[pltpu.VMEM(s, t) for s, t in scratch],
        compiler_params=pltpu.CompilerParams(vmem_limit_bytes=32 * 1024 * 1024),
    )


def shape(dims, dtype=BF16):
    return jax.ShapeDtypeStruct(dims, dtype)


def holders(turned):
    def at(y, z):
        return y * 4 + z

    inner, outer = ((0, 1), (2, 3)) if turned else ((2, 3), (0, 1))
    low = [at(half + y, z) for half in (0, 4) for y in outer for z in (0, 1)]
    high = [at(half + y, z) for half in (0, 4) for y in outer for z in (3, 2)]
    within = [at(half + y, z) for half in (0, 4) for y in inner for z in range(4)]
    return high + within + low if turned else low + within + high


def is_turned(patch):
    return patch % 2 == 1, patch % 8 != 7


def member_order():
    return [15, 14, 27, 26, 11, 10, 31, 30, 19, 23, 18, 22, 0, 1, 4, 5, 16, 17, 20, 21, 3, 2, 7, 6, 8, 9, 12, 13, 24, 25, 28, 29]


def return_order():
    return [18, 19, 22, 23, 2, 3, 6, 7, 0, 4, 28, 1, 5, 29, 8, 24, 9, 25, 10, 11, 12, 13, 14, 15, 16, 17, 20, 21, 26, 27, 30, 31]


def places(order):
    odd, near = is_turned(lax.axis_index("patch"))
    turned = jnp.logical_and(odd, near)
    return [
        jnp.where(turned, order.index(there), order.index(here))
        for here, there in zip(holders(False), holders(True))
    ]


def groups(patches):
    cells, returns = (
        [[m * patches + p for m in order] for p in range(patches)]
        for order in (member_order(), return_order())
    )
    held = [[m * patches + p for m in holders(all(is_turned(p)))] for p in range(patches)]
    windows = []
    for p in range(patches):
        here, east = held[p], held[(p + 1) % patches]
        windows += [here[8:16], here[16:24]]
        windows += [here[24:28] + east[0:4], here[28:32] + east[4:8]]
    return cells, windows, returns


def exchange(array, parties):
    return lax.all_to_all(
        array, ("member", "patch"), 0, 0, axis_index_groups=parties, tiled=True
    )


def body(
    state_field, cotangent, obs_count, member_gain, spatial_gain, member_weights, spatial_weights
):
    cells, windows, returns = groups(lax.axis_size("patch"))
    member_gain, spatial_gain = member_gain.reshape(1, D), spatial_gain.reshape(1, D)
    rows = (ROWS, D)
    sent = pl.pallas_call(
        spread_kernel,
        out_shape=shape((32, 16, D)),
        in_specs=[pl.BlockSpec(memory_space=pltpu.HBM)] * 3,
        scratch_shapes=[
            pltpu.VMEM((16, 16, D), BF16),
            pltpu.VMEM((16, 16, D), BF16),
            pltpu.VMEM((16, 16), jnp.int32),
            pltpu.SemaphoreType.DMA((3,)),
        ],
        compiler_params=pltpu.CompilerParams(vmem_limit_bytes=32 * 1024 * 1024),
    )(
        *(
            pltpu.with_memory_space_constraint(array, pltpu.HBM)
            for array in (state_field.reshape(16, 16, D), cotangent.reshape(16, 16, D), obs_count)
        )
    )
    at_cells = exchange(sent, cells)
    hidden, state, q, k, v, probs = call(
        member_forward_kernel,
        [shape((8, 4, 16, D))] + [shape(rows)] * 4 + [shape((8, 32, 256), F32)],
        [(rows, BF16)],
    )(at_cells, member_gain, member_weights)
    at_windows = exchange(hidden, windows)
    grads = call(window_kernel, shape((8, 4, 8, D)), [(rows, BF16)] * 7)(
        at_windows, spatial_gain, spatial_weights
    )
    back_at_cells = exchange(grads, windows)
    field = call(member_backward_kernel, shape((32, 8, D)), [(rows, BF16)] * 4)(
        back_at_cells, state, q, k, v, probs, member_gain, member_weights
    )
    returned = exchange(field, returns)
    out = call(gather_kernel, shape((16, 16, D)))(returned)
    return out.reshape(1, 16, 16, D)


def solution(mesh):
    placed = (
        P("member", None, "patch", None),
        P("member", None, "patch", None),
        P(None, "patch"),
        P(),
        P(),
        P(),
        P(),
    )
    return jax.shard_map(
        body,
        mesh=mesh,
        in_specs=placed,
        out_specs=P("member", None, "patch", None),
        check_vma=False,
    )
```

```python
import jax
import jax.numpy as jnp
from jax import lax
from jax.experimental import pallas as pl
from jax.experimental.pallas import tpu as pltpu
from jax.sharding import PartitionSpec as P

F32 = jnp.float32
BF16 = jnp.bfloat16
D = 512
PAIRS = 4
SCALE = 64 ** (-0.5)
EPS = 1e-6
ROWS = 256
BLOCK = 128

NN = (((1,), (0,)), ((), ()))
NT = (((1,), (1,)), ((), ()))
TN = (((0,), (0,)), ((), ()))


def dot(a, b, dims=NN):
    return lax.dot_general(a, b, dims, preferred_element_type=F32)


def inverse_rms(values):
    return lax.rsqrt(jnp.mean(values * values, axis=-1, keepdims=True) + EPS)


def norm_back(values, inverse, gain, upstream):
    scaled = gain * upstream
    inner = jnp.mean(scaled * values, axis=-1, keepdims=True)
    return inverse * scaled - values * (inverse * inverse * inverse * inner)


def cell_major():
    to = lax.broadcasted_iota(jnp.int32, (ROWS, ROWS), 0)
    at = lax.broadcasted_iota(jnp.int32, (ROWS, ROWS), 1)
    return (at == (to % 32) * 8 + to // 32).astype(F32).astype(BF16)


def member_major():
    to = lax.broadcasted_iota(jnp.int32, (ROWS, ROWS), 0)
    at = lax.broadcasted_iota(jnp.int32, (ROWS, ROWS), 1)
    return (at == (to % 8) * 32 + to // 8).astype(F32).astype(BF16)


def head_split(rows):
    first = lax.broadcasted_iota(jnp.int32, rows.shape, 1) < 64
    zero = jnp.zeros_like(rows)
    return jnp.concatenate([jnp.where(first, rows, zero), jnp.where(first, zero, rows)], axis=0)


def head_join(stacked):
    first = lax.broadcasted_iota(jnp.int32, (BLOCK, 128), 1) < 64
    return jnp.where(first, stacked[:BLOCK], stacked[BLOCK:])


def own_group(width, size):
    return (lax.broadcasted_iota(jnp.int32, (size, width), 1) % BLOCK) // size


def compact(full, size):
    group = own_group(full.shape[1], size)
    kept = full[:size]
    for g in range(1, BLOCK // size):
        kept = jnp.where(group == g, full[g * size : (g + 1) * size], kept)
    return kept


def expand(kept, size):
    group = own_group(kept.shape[1], size)
    zero = jnp.zeros_like(kept)
    return jnp.concatenate(
        [jnp.where(group == g, kept, zero) for g in range(BLOCK // size)], axis=0
    ).astype(BF16)


def softmax_keys(scores):
    raised = jnp.exp(scores - jnp.max(scores, axis=0, keepdims=True))
    return raised * (1.0 / jnp.sum(raised, axis=0, keepdims=True))


def blocks():
    return [
        (slice(b * BLOCK, (b + 1) * BLOCK), slice(p * 128, (p + 1) * 128))
        for b in range(ROWS // BLOCK)
        for p in range(PAIRS)
    ]


def attention_probs(q_split, k_ref, size):
    scores = [dot(k_ref[at], q, NT) for at, q in zip(blocks(), q_split)]
    scores = [compact(s, size) * SCALE for s in scores]
    return [softmax_keys(s) for s in scores]


def attention_backward(probs, q_split, k_ref, v_ref, do_split, dq_ref, dk_ref, dv_ref, size):
    grads = [dot(v_ref[at], do, NT) for at, do in zip(blocks(), do_split)]
    grads = [compact(g, size) for g in grads]
    wide = [expand(p, size) for p in probs]
    ds = [
        expand(p * (g - jnp.sum(p * g, axis=0, keepdims=True)) * SCALE, size)
        for p, g in zip(probs, grads)
    ]
    for at, p, do in zip(blocks(), wide, do_split):
        dv_ref[at] = dot(p, do).astype(BF16)
    for at, d, q in zip(blocks(), ds, q_split):
        dk_ref[at] = dot(d, q).astype(BF16)
    for at, d in zip(blocks(), ds):
        dq_ref[at] = head_join(dot(d, k_ref[at], TN)).astype(BF16)


def spread_kernel(state_hbm, cot_hbm, obs_hbm, out_ref, state_ref, cot_ref, obs_ref, sems):
    copies = [
        pltpu.make_async_copy(src, dst, sems.at[i])
        for i, (src, dst) in enumerate(
            ((obs_hbm, obs_ref), (state_hbm, state_ref), (cot_hbm, cot_ref))
        )
    ]
    for copy in copies:
        copy.start()
    for copy in copies:
        copy.wait()
    obs = obs_ref[...].astype(F32)
    eye = lax.broadcasted_iota(jnp.int32, (16, 16, 16), 1) == lax.broadcasted_iota(
        jnp.int32, (16, 16, 16), 2
    )
    weight = jnp.sum(jnp.where(eye, obs[:, None, :], 0.0), axis=-1, keepdims=True)
    dy = cot_ref[...].astype(F32) * weight
    parts = []
    for values in (state_ref[...].astype(F32), dy):
        inner = values[:, 4:12]
        west = values[:, 0:4].reshape(8, 2, 4, D)
        east = values[:, 12:16].reshape(8, 2, 4, D)
        parts.append(
            [
                jnp.concatenate([west[:, 0], west[:, 1]], axis=1),
                inner,
                jnp.concatenate([east[:, 0], east[:, 1]], axis=1),
            ]
        )
    sent = [jnp.concatenate([a, b], axis=1).astype(BF16) for a, b in zip(parts[0], parts[1])]
    sent = jnp.concatenate(sent, axis=0)
    for block, at in enumerate(places(member_order())):
        out_ref[at] = sent[block]


def gather_kernel(in_ref, out_ref):
    values = jnp.stack([in_ref[at] for at in places(return_order())]).astype(F32)
    west, east = values[0:8], values[24:32]
    inner = values[8:24].reshape(8, 2, 8, D)
    rows = [
        jnp.concatenate([west[:, 4 * i : 4 * i + 4], inner[:, i], east[:, 4 * i : 4 * i + 4]], axis=1)
        for i in range(2)
    ]
    out_ref[...] = jnp.stack(rows, axis=1).reshape(16, 16, D).astype(BF16)


def member_forward_kernel(
    in_ref, gain_ref, w_ref, out_ref, state_ref, q_ref, k_ref, v_ref, probs_ref, attended_ref
):
    values = in_ref[...].astype(F32)
    state = dot(cell_major(), values[:, :8].reshape(ROWS, D).astype(BF16))
    state_ref[...] = state.astype(BF16)
    normed = (state * inverse_rms(state) * gain_ref[...]).astype(BF16)
    q_ref[...] = dot(normed, w_ref[0]).astype(BF16)
    k_ref[...] = dot(normed, w_ref[1]).astype(BF16)
    v_ref[...] = dot(normed, w_ref[2]).astype(BF16)
    probs = attention_probs([head_split(q_ref[at]) for at in blocks()], k_ref, 32)
    for i, p in enumerate(probs):
        probs_ref[i] = p
    for at, p in zip(blocks(), probs):
        attended_ref[at] = head_join(dot(expand(p, 32), v_ref[at], TN)).astype(BF16)
    hidden = (state + dot(attended_ref[...], w_ref[3])).astype(BF16)
    hidden = dot(member_major(), hidden).reshape(32, 8, D)
    out_ref[...] = jnp.concatenate([hidden, values[:, 8:]], axis=1).astype(BF16).reshape(8, 4, 16, D)


def window_kernel(
    in_ref, gain_ref, w_ref, out_ref, q_ref, k_ref, v_ref, do_ref, dq_ref, dk_ref, dv_ref
):
    values = in_ref[...].astype(F32)
    hidden = jnp.concatenate([values[:, m, :8].reshape(64, D) for m in range(4)], axis=0)
    dy = jnp.concatenate([values[:, m, 8:].reshape(64, D) for m in range(4)], axis=0)
    inverse = inverse_rms(hidden)
    normed = (hidden * inverse * gain_ref[...]).astype(BF16)
    q_ref[...] = dot(normed, w_ref[0]).astype(BF16)
    k_ref[...] = dot(normed, w_ref[1]).astype(BF16)
    v_ref[...] = dot(normed, w_ref[2]).astype(BF16)
    do_ref[...] = dot(dy.astype(BF16), w_ref[3], NT).astype(BF16)
    q_split = [head_split(q_ref[at]) for at in blocks()]
    do_split = [head_split(do_ref[at]) for at in blocks()]
    probs = attention_probs(q_split, k_ref, 64)
    attention_backward(probs, q_split, k_ref, v_ref, do_split, dq_ref, dk_ref, dv_ref, 64)
    upstream = (
        dot(dq_ref[...], w_ref[0], NT) + dot(dk_ref[...], w_ref[1], NT) + dot(dv_ref[...], w_ref[2], NT)
    )
    grad = dy + norm_back(hidden, inverse, gain_ref[...], upstream)
    for m in range(4):
        out_ref[:, m] = grad[m * 64 : (m + 1) * 64].reshape(8, 8, D).astype(BF16)


def member_backward_kernel(
    in_ref, state_ref, q_ref, k_ref, v_ref, probs_ref, gain_ref, w_ref, out_ref, do_ref, dq_ref, dk_ref, dv_ref
):
    values = in_ref[...].astype(F32).reshape(ROWS, D).astype(BF16)
    hidden_grad = dot(cell_major(), values)
    do_ref[...] = dot(hidden_grad.astype(BF16), w_ref[3], NT).astype(BF16)
    q_split = [head_split(q_ref[at]) for at in blocks()]
    do_split = [head_split(do_ref[at]) for at in blocks()]
    probs = [probs_ref[i] for i in range(len(q_split))]
    attention_backward(probs, q_split, k_ref, v_ref, do_split, dq_ref, dk_ref, dv_ref, 32)
    upstream = (
        dot(dq_ref[...], w_ref[0], NT) + dot(dk_ref[...], w_ref[1], NT) + dot(dv_ref[...], w_ref[2], NT)
    )
    state = state_ref[...].astype(F32)
    grad = (hidden_grad + norm_back(state, inverse_rms(state), gain_ref[...], upstream)).astype(BF16)
    grad = dot(member_major(), grad).reshape(32, 8, D).astype(BF16)
    order = member_order()
    for k, m in enumerate(return_order()):
        out_ref[k] = grad[order.index(m)]


def call(kernel, outs, scratch=()):
    return pl.pallas_call(
        kernel,
        out_shape=outs,
        scratch_shapes=[pltpu.VMEM(s, t) for s, t in scratch],
        compiler_params=pltpu.CompilerParams(vmem_limit_bytes=32 * 1024 * 1024),
    )


def shape(dims, dtype=BF16):
    return jax.ShapeDtypeStruct(dims, dtype)


def holders(turned):
    def at(y, z):
        return y * 4 + z

    inner, outer = ((0, 1), (2, 3)) if turned else ((2, 3), (0, 1))
    low = [at(half + y, z) for half in (0, 4) for y in outer for z in (0, 1)]
    high = [at(half + y, z) for half in (0, 4) for y in outer for z in (3, 2)]
    within = [at(half + y, z) for half in (0, 4) for y in inner for z in range(4)]
    return high + within + low if turned else low + within + high


def is_turned(patch):
    return patch % 2 == 1, patch % 8 != 7


def member_order():
    return [15, 27, 11, 31, 14, 26, 10, 30, 19, 23, 18, 22, 4, 0, 5, 1, 20, 16, 21, 17, 7, 3, 6, 2, 8, 9, 12, 13, 24, 25, 28, 29]


def return_order():
    return [18, 19, 22, 23, 2, 3, 6, 7, 0, 4, 28, 1, 5, 29, 8, 24, 9, 25, 10, 11, 12, 13, 14, 15, 16, 17, 20, 21, 26, 27, 30, 31]


def places(order):
    odd, near = is_turned(lax.axis_index("patch"))
    turned = jnp.logical_and(odd, near)
    return [
        jnp.where(turned, order.index(there), order.index(here))
        for here, there in zip(holders(False), holders(True))
    ]


def groups(patches):
    cells, returns = (
        [[m * patches + p for m in order] for p in range(patches)]
        for order in (member_order(), return_order())
    )
    held = [[m * patches + p for m in holders(all(is_turned(p)))] for p in range(patches)]
    windows = []
    for p in range(patches):
        here, east = held[p], held[(p + 1) % patches]
        windows += [here[8:16], here[16:24]]
        windows += [here[24:28] + east[0:4], here[28:32] + east[4:8]]
    return cells, windows, returns


def exchange(array, parties):
    return lax.all_to_all(
        array, ("member", "patch"), 0, 0, axis_index_groups=parties, tiled=True
    )


def body(
    state_field, cotangent, obs_count, member_gain, spatial_gain, member_weights, spatial_weights
):
    cells, windows, returns = groups(lax.axis_size("patch"))
    member_gain, spatial_gain = member_gain.reshape(1, D), spatial_gain.reshape(1, D)
    rows = (ROWS, D)
    sent = pl.pallas_call(
        spread_kernel,
        out_shape=shape((32, 16, D)),
        in_specs=[pl.BlockSpec(memory_space=pltpu.HBM)] * 3,
        scratch_shapes=[
            pltpu.VMEM((16, 16, D), BF16),
            pltpu.VMEM((16, 16, D), BF16),
            pltpu.VMEM((16, 16), jnp.int32),
            pltpu.SemaphoreType.DMA((3,)),
        ],
        compiler_params=pltpu.CompilerParams(vmem_limit_bytes=32 * 1024 * 1024),
    )(
        *(
            pltpu.with_memory_space_constraint(array, pltpu.HBM)
            for array in (state_field.reshape(16, 16, D), cotangent.reshape(16, 16, D), obs_count)
        )
    )
    at_cells = exchange(sent, cells)
    hidden, state, q, k, v, probs = call(
        member_forward_kernel,
        [shape((8, 4, 16, D))] + [shape(rows)] * 4 + [shape((8, 32, 256), F32)],
        [(rows, BF16)],
    )(at_cells, member_gain, member_weights)
    at_windows = exchange(hidden, windows)
    grads = call(window_kernel, shape((8, 4, 8, D)), [(rows, BF16)] * 7)(
        at_windows, spatial_gain, spatial_weights
    )
    back_at_cells = exchange(grads, windows)
    field = call(member_backward_kernel, shape((32, 8, D)), [(rows, BF16)] * 4)(
        back_at_cells, state, q, k, v, probs, member_gain, member_weights
    )
    returned = exchange(field, returns)
    out = call(gather_kernel, shape((16, 16, D)))(returned)
    return out.reshape(1, 16, 16, D)


def solution(mesh):
    placed = (
        P("member", None, "patch", None),
        P("member", None, "patch", None),
        P(None, "patch"),
        P(),
        P(),
        P(),
        P(),
    )
    return jax.shard_map(
        body,
        mesh=mesh,
        in_specs=placed,
        out_specs=P("member", None, "patch", None),
        check_vma=False,
    )
```

```python
import jax
import jax.numpy as jnp
from jax import lax
from jax.experimental import pallas as pl
from jax.experimental.pallas import tpu as pltpu
from jax.sharding import PartitionSpec as P

F32 = jnp.float32
BF16 = jnp.bfloat16
D = 512
PAIRS = 4
SCALE = 64 ** (-0.5)
EPS = 1e-6
ROWS = 256
BLOCK = 128

NN = (((1,), (0,)), ((), ()))
NT = (((1,), (1,)), ((), ()))
TN = (((0,), (0,)), ((), ()))


def dot(a, b, dims=NN):
    return lax.dot_general(a, b, dims, preferred_element_type=F32)


def inverse_rms(values):
    return lax.rsqrt(jnp.mean(values * values, axis=-1, keepdims=True) + EPS)


def norm_back(values, inverse, gain, upstream):
    scaled = gain * upstream
    inner = jnp.mean(scaled * values, axis=-1, keepdims=True)
    return inverse * scaled - values * (inverse * inverse * inverse * inner)


def cell_major():
    to = lax.broadcasted_iota(jnp.int32, (ROWS, ROWS), 0)
    at = lax.broadcasted_iota(jnp.int32, (ROWS, ROWS), 1)
    return (at == (to % 32) * 8 + to // 32).astype(F32).astype(BF16)


def member_major():
    to = lax.broadcasted_iota(jnp.int32, (ROWS, ROWS), 0)
    at = lax.broadcasted_iota(jnp.int32, (ROWS, ROWS), 1)
    return (at == (to % 8) * 32 + to // 8).astype(F32).astype(BF16)


def head_split(rows):
    first = lax.broadcasted_iota(jnp.int32, rows.shape, 1) < 64
    zero = jnp.zeros_like(rows)
    return jnp.concatenate([jnp.where(first, rows, zero), jnp.where(first, zero, rows)], axis=0)


def head_join(stacked):
    first = lax.broadcasted_iota(jnp.int32, (BLOCK, 128), 1) < 64
    return jnp.where(first, stacked[:BLOCK], stacked[BLOCK:])


def own_group(width, size):
    return (lax.broadcasted_iota(jnp.int32, (size, width), 1) % BLOCK) // size


def compact(full, size):
    group = own_group(full.shape[1], size)
    kept = full[:size]
    for g in range(1, BLOCK // size):
        kept = jnp.where(group == g, full[g * size : (g + 1) * size], kept)
    return kept


def expand(kept, size):
    group = own_group(kept.shape[1], size)
    zero = jnp.zeros_like(kept)
    return jnp.concatenate(
        [jnp.where(group == g, kept, zero) for g in range(BLOCK // size)], axis=0
    ).astype(BF16)


def softmax_keys(scores):
    raised = jnp.exp(scores - jnp.max(scores, axis=0, keepdims=True))
    return raised * (1.0 / jnp.sum(raised, axis=0, keepdims=True))


def blocks():
    return [
        (slice(b * BLOCK, (b + 1) * BLOCK), slice(p * 128, (p + 1) * 128))
        for b in range(ROWS // BLOCK)
        for p in range(PAIRS)
    ]


def attention_probs(q_split, k_ref, size):
    scores = [dot(k_ref[at], q, NT) for at, q in zip(blocks(), q_split)]
    scores = [compact(s, size) * SCALE for s in scores]
    return [softmax_keys(s) for s in scores]


def attention_backward(probs, q_split, k_ref, v_ref, do_split, dq_ref, dk_ref, dv_ref, size):
    grads = [dot(v_ref[at], do, NT) for at, do in zip(blocks(), do_split)]
    grads = [compact(g, size) for g in grads]
    wide = [expand(p, size) for p in probs]
    ds = [
        expand(p * (g - jnp.sum(p * g, axis=0, keepdims=True)) * SCALE, size)
        for p, g in zip(probs, grads)
    ]
    for at, p, do in zip(blocks(), wide, do_split):
        dv_ref[at] = dot(p, do).astype(BF16)
    for at, d, q in zip(blocks(), ds, q_split):
        dk_ref[at] = dot(d, q).astype(BF16)
    for at, d in zip(blocks(), ds):
        dq_ref[at] = head_join(dot(d, k_ref[at], TN)).astype(BF16)


def spread_kernel(state_hbm, cot_hbm, obs_hbm, out_ref, state_ref, cot_ref, obs_ref, sems):
    copies = [
        pltpu.make_async_copy(src, dst, sems.at[i])
        for i, (src, dst) in enumerate(
            ((obs_hbm, obs_ref), (state_hbm, state_ref), (cot_hbm, cot_ref))
        )
    ]
    for copy in copies:
        copy.start()
    copies[0].wait()
    obs = obs_ref[...].astype(F32)
    eye = lax.broadcasted_iota(jnp.int32, (16, 16, 16), 1) == lax.broadcasted_iota(
        jnp.int32, (16, 16, 16), 2
    )
    weight = jnp.sum(jnp.where(eye, obs[:, None, :], 0.0), axis=-1, keepdims=True)
    parts = []
    for ref, copy, scale in ((state_ref, copies[1], None), (cot_ref, copies[2], weight)):
        copy.wait()
        values = ref[...].astype(F32)
        if scale is not None:
            values = values * scale
        inner = values[:, 4:12]
        west = values[:, 0:4].reshape(8, 2, 4, D)
        east = values[:, 12:16].reshape(8, 2, 4, D)
        parts.append(
            [
                jnp.concatenate([west[:, 0], west[:, 1]], axis=1),
                inner,
                jnp.concatenate([east[:, 0], east[:, 1]], axis=1),
            ]
        )
    sent = [jnp.concatenate([a, b], axis=1).astype(BF16) for a, b in zip(parts[0], parts[1])]
    sent = jnp.concatenate(sent, axis=0)
    for block, at in enumerate(places(member_order())):
        out_ref[at] = sent[block]


def gather_kernel(in_ref, out_ref):
    values = jnp.stack([in_ref[at] for at in places(return_order())]).astype(F32)
    west, east = values[0:8], values[24:32]
    inner = values[8:24].reshape(8, 2, 8, D)
    rows = [
        jnp.concatenate([west[:, 4 * i : 4 * i + 4], inner[:, i], east[:, 4 * i : 4 * i + 4]], axis=1)
        for i in range(2)
    ]
    out_ref[...] = jnp.stack(rows, axis=1).reshape(16, 16, D).astype(BF16)


def member_forward_kernel(
    in_ref, gain_ref, w_ref, out_ref, state_ref, q_ref, k_ref, v_ref, probs_ref, attended_ref
):
    values = in_ref[...].astype(F32)
    state = dot(cell_major(), values[:, :8].reshape(ROWS, D).astype(BF16))
    state_ref[...] = state.astype(BF16)
    normed = (state * inverse_rms(state) * gain_ref[...]).astype(BF16)
    q_ref[...] = dot(normed, w_ref[0]).astype(BF16)
    k_ref[...] = dot(normed, w_ref[1]).astype(BF16)
    v_ref[...] = dot(normed, w_ref[2]).astype(BF16)
    probs = attention_probs([head_split(q_ref[at]) for at in blocks()], k_ref, 32)
    for i, p in enumerate(probs):
        probs_ref[i] = p
    for at, p in zip(blocks(), probs):
        attended_ref[at] = head_join(dot(expand(p, 32), v_ref[at], TN)).astype(BF16)
    hidden = (state + dot(attended_ref[...], w_ref[3])).astype(BF16)
    hidden = dot(member_major(), hidden).reshape(32, 8, D)
    out_ref[...] = jnp.concatenate([hidden, values[:, 8:]], axis=1).astype(BF16).reshape(8, 4, 16, D)


def window_kernel(
    in_ref, gain_ref, w_ref, out_ref, q_ref, k_ref, v_ref, do_ref, dq_ref, dk_ref, dv_ref
):
    values = in_ref[...].astype(F32)
    hidden = jnp.concatenate([values[:, m, :8].reshape(64, D) for m in range(4)], axis=0)
    dy = jnp.concatenate([values[:, m, 8:].reshape(64, D) for m in range(4)], axis=0)
    inverse = inverse_rms(hidden)
    normed = (hidden * inverse * gain_ref[...]).astype(BF16)
    q_ref[...] = dot(normed, w_ref[0]).astype(BF16)
    k_ref[...] = dot(normed, w_ref[1]).astype(BF16)
    v_ref[...] = dot(normed, w_ref[2]).astype(BF16)
    do_ref[...] = dot(dy.astype(BF16), w_ref[3], NT).astype(BF16)
    q_split = [head_split(q_ref[at]) for at in blocks()]
    do_split = [head_split(do_ref[at]) for at in blocks()]
    probs = attention_probs(q_split, k_ref, 64)
    attention_backward(probs, q_split, k_ref, v_ref, do_split, dq_ref, dk_ref, dv_ref, 64)
    upstream = (
        dot(dq_ref[...], w_ref[0], NT) + dot(dk_ref[...], w_ref[1], NT) + dot(dv_ref[...], w_ref[2], NT)
    )
    grad = dy + norm_back(hidden, inverse, gain_ref[...], upstream)
    for m in range(4):
        out_ref[:, m] = grad[m * 64 : (m + 1) * 64].reshape(8, 8, D).astype(BF16)


def member_backward_kernel(
    in_ref, state_ref, q_ref, k_ref, v_ref, probs_ref, gain_ref, w_ref, out_ref, do_ref, dq_ref, dk_ref, dv_ref
):
    values = in_ref[...].astype(F32).reshape(ROWS, D).astype(BF16)
    hidden_grad = dot(cell_major(), values)
    do_ref[...] = dot(hidden_grad.astype(BF16), w_ref[3], NT).astype(BF16)
    q_split = [head_split(q_ref[at]) for at in blocks()]
    do_split = [head_split(do_ref[at]) for at in blocks()]
    probs = [probs_ref[i] for i in range(len(q_split))]
    attention_backward(probs, q_split, k_ref, v_ref, do_split, dq_ref, dk_ref, dv_ref, 32)
    upstream = (
        dot(dq_ref[...], w_ref[0], NT) + dot(dk_ref[...], w_ref[1], NT) + dot(dv_ref[...], w_ref[2], NT)
    )
    state = state_ref[...].astype(F32)
    grad = (hidden_grad + norm_back(state, inverse_rms(state), gain_ref[...], upstream)).astype(BF16)
    grad = dot(member_major(), grad).reshape(32, 8, D).astype(BF16)
    order = member_order()
    for k, m in enumerate(return_order()):
        out_ref[k] = grad[order.index(m)]


def call(kernel, outs, scratch=()):
    return pl.pallas_call(
        kernel,
        out_shape=outs,
        scratch_shapes=[pltpu.VMEM(s, t) for s, t in scratch],
        compiler_params=pltpu.CompilerParams(vmem_limit_bytes=32 * 1024 * 1024),
    )


def shape(dims, dtype=BF16):
    return jax.ShapeDtypeStruct(dims, dtype)


def holders(turned):
    def at(y, z):
        return y * 4 + z

    inner, outer = ((0, 1), (2, 3)) if turned else ((2, 3), (0, 1))
    low = [at(half + y, z) for half in (0, 4) for y in outer for z in (0, 1)]
    high = [at(half + y, z) for half in (0, 4) for y in outer for z in (3, 2)]
    within = [at(half + y, z) for half in (0, 4) for y in inner for z in range(4)]
    return high + within + low if turned else low + within + high


def is_turned(patch):
    return patch % 2 == 1, patch % 8 != 7


def member_order():
    return [15, 27, 11, 31, 14, 26, 10, 30, 19, 23, 18, 22, 4, 0, 5, 1, 20, 16, 21, 17, 7, 3, 6, 2, 8, 9, 12, 13, 24, 25, 28, 29]


def return_order():
    return [18, 19, 22, 23, 2, 3, 6, 7, 0, 4, 28, 1, 5, 29, 8, 24, 9, 25, 10, 11, 12, 13, 14, 15, 16, 17, 20, 21, 26, 27, 30, 31]


def places(order):
    odd, near = is_turned(lax.axis_index("patch"))
    turned = jnp.logical_and(odd, near)
    return [
        jnp.where(turned, order.index(there), order.index(here))
        for here, there in zip(holders(False), holders(True))
    ]


def groups(patches):
    cells, returns = (
        [[m * patches + p for m in order] for p in range(patches)]
        for order in (member_order(), return_order())
    )
    held = [[m * patches + p for m in holders(all(is_turned(p)))] for p in range(patches)]
    windows = []
    for p in range(patches):
        here, east = held[p], held[(p + 1) % patches]
        windows += [here[8:16], here[16:24]]
        for half in (0, 4):
            both = here[24 + half : 28 + half], east[half : half + 4]
            windows.append([group[i] for group in both for i in (1, 3, 0, 2)])
    return cells, windows, returns


def exchange(array, parties):
    return lax.all_to_all(
        array, ("member", "patch"), 0, 0, axis_index_groups=parties, tiled=True
    )


def body(
    state_field, cotangent, obs_count, member_gain, spatial_gain, member_weights, spatial_weights
):
    cells, windows, returns = groups(lax.axis_size("patch"))
    member_gain, spatial_gain = member_gain.reshape(1, D), spatial_gain.reshape(1, D)
    rows = (ROWS, D)
    sent = pl.pallas_call(
        spread_kernel,
        out_shape=shape((32, 16, D)),
        in_specs=[pl.BlockSpec(memory_space=pltpu.HBM)] * 3,
        scratch_shapes=[
            pltpu.VMEM((16, 16, D), BF16),
            pltpu.VMEM((16, 16, D), BF16),
            pltpu.VMEM((16, 16), jnp.int32),
            pltpu.SemaphoreType.DMA((3,)),
        ],
        compiler_params=pltpu.CompilerParams(vmem_limit_bytes=32 * 1024 * 1024),
    )(
        *(
            pltpu.with_memory_space_constraint(array, pltpu.HBM)
            for array in (state_field.reshape(16, 16, D), cotangent.reshape(16, 16, D), obs_count)
        )
    )
    at_cells = exchange(sent, cells)
    hidden, state, q, k, v, probs = call(
        member_forward_kernel,
        [shape((8, 4, 16, D))] + [shape(rows)] * 4 + [shape((8, 32, 256), F32)],
        [(rows, BF16)],
    )(at_cells, member_gain, member_weights)
    at_windows = exchange(hidden, windows)
    grads = call(window_kernel, shape((8, 4, 8, D)), [(rows, BF16)] * 7)(
        at_windows, spatial_gain, spatial_weights
    )
    back_at_cells = exchange(grads, windows)
    field = call(member_backward_kernel, shape((32, 8, D)), [(rows, BF16)] * 4)(
        back_at_cells, state, q, k, v, probs, member_gain, member_weights
    )
    returned = exchange(field, returns)
    out = call(gather_kernel, shape((16, 16, D)))(returned)
    return out.reshape(1, 16, 16, D)


def solution(mesh):
    placed = (
        P("member", None, "patch", None),
        P("member", None, "patch", None),
        P(None, "patch"),
        P(),
        P(),
        P(),
        P(),
    )
    return jax.shard_map(
        body,
        mesh=mesh,
        in_specs=placed,
        out_specs=P("member", None, "patch", None),
        check_vma=False,
    )
```
